128 devices in a mesh: blk: 32 (over x, y, z_hi), ha: 4 (over z_lo, core).
Axes of the slice: x: 4, y: 4, z: 4 (z_hi: 2, z_lo: 2; z = z_hi * 2 + z_lo), core: 2. Of those that a mesh axis runs over, the one named last changes fastest.
Arguments:
- int_temp: float32 [32, 1024, 1024], P(None, 'blk', 'ha'), may hold values from 0.5 to 3
- int_degree: float32 [32, 1024, 1024], P(None, 'blk', 'ha'), may hold values from 0.05 to 0.6
- int_affinity: float32 [32, 1024, 1024], P(None, 'blk', 'ha'), may hold values from 0.02 to 0.15
- skin_humidity: float32 [16, 256, 8192], P(None, 'ha', 'blk'), may hold values from 0.6 to 1
- skin_temp: float32 [16, 256, 8192], P(None, 'ha', 'blk'), may hold values from 0 to 2
- skin_degree: float32 [16, 256, 8192], P(None, 'ha', 'blk'), may hold values from 0.05 to 0.6
- ambient: float32 [256, 8192], P('ha', 'blk'), may hold values from 0.4 to 0.8
- colmap: int32 [8192], P('blk'), may hold values from 0 to 16383, as said below
Outputs:
- int_temp_out: float32 [32, 1024, 1024], P(None, 'blk', 'ha')
- int_degree_out: float32 [32, 1024, 1024], P(None, 'blk', 'ha')
- skin_humidity_out: float32 [16, 256, 8192], P(None, 'ha', 'blk')
- skin_temp_out: float32 [16, 256, 8192], P(None, 'ha', 'blk')
The draws below stay inside these ranges and needn't reach their ends.
Inputs may be any that keep to these rules, and one draw needn't show every extreme that they name: `colmap`: coarse column c belongs to device c // 128 of blk+ha. Among the 256 arcs of one device at most 4 name columns of any one device, and in every draw one device has exactly 4 arcs of every device's arcs naming its columns.
All inputs are finite; a program needn't handle non-finite values.
Results may differ from the reference program's by a relative error of at most 0.00009.
Values sent between devices are 32-bit elements; how exact they have to be, the bound alone decides.
A program may use at most 128 MiB of HBM per device.

```python
import math
import jax
import jax.numpy as jnp

IX = 32
IY = 256
NZ = 32
CB = 8
INT_STEPS = 2
ARCS = 256
DEPTH = 16
SUB = 4
COLS_DEV = 128
NCOL = 16384
CAP = 4
NXI = 1024
NYI = 1024
HS = 256
PER = 8192
N_BLK = 32
N_HA = 4
DEVICES = 128


def draw_colmap(key, part):
    key = jax.random.fold_in(key, 11)
    keys = jax.random.split(key, 3)
    common = jax.random.randint(keys[0], (), 0, DEVICES).astype(jnp.int32)
    slots = ARCS // CAP

    def one_block(block_key):
        key_perm, key_cut, key_pos = jax.random.split(block_key, 3)
        others = jax.random.permutation(key_perm, DEVICES - 1).astype(jnp.int32)
        others = others + (others >= common).astype(jnp.int32)
        cuts = jax.random.randint(key_cut, (slots,), 1, CAP + 1).astype(jnp.int32)
        cuts = cuts.at[0].set(CAP)
        position = jax.random.permutation(key_pos, ARCS).astype(jnp.int32)
        slot_of = position // CAP
        offset = position % CAP
        primary = jnp.concatenate([common[None], others[:slots - 1]])
        spill = jnp.concatenate([common[None], others[slots - 1:2 * slots - 2]])
        return jnp.where(offset < cuts[slot_of], primary[slot_of], spill[slot_of])
    owners = jax.vmap(one_block)(jax.random.split(keys[1], N_BLK)).reshape(PER)
    local_col = jax.random.randint(keys[2], (PER,), 0, COLS_DEV).astype(jnp.int32)
    return (owners * COLS_DEV + local_col).astype(jnp.int32)


def levels(rng, extent, shards, least, largest):
    level, own = 1.0, jax.random.fold_in(rng, 6)
    for dim, shards_of in shards:
        steps = jnp.exp(jax.random.uniform(jax.random.fold_in(own, dim), (shards_of,), jnp.float32, least / len(shards), largest / len(shards)))
        level = level * jnp.repeat(steps, extent[dim] // shards_of).reshape([-1 if axis == dim else 1 for axis in range(len(extent))])
    return level


def setup_inputs(seed: int = 0) -> dict:
    streams_of = jax.random.split(jax.random.key(seed), 9)
    return {
        "int_temp": jnp.clip(0.5 + 2.5 * jax.random.uniform(streams_of[0], (NZ, NXI, NYI), jnp.float32) ** levels(streams_of[0], (NZ, NXI, NYI), ((1, 32), (2, 4)), -0.2, 0.2), 0.5, 3.0),
        "int_degree": jnp.clip(0.05 + 0.55 * jax.random.uniform(streams_of[1], (NZ, NXI, NYI), jnp.float32) ** levels(streams_of[1], (NZ, NXI, NYI), ((1, 32), (2, 4)), -0.2, 0.2), 0.05, 0.6),
        "int_affinity": jnp.clip(jnp.exp(math.log(0.15) - 2.014903 * jax.random.uniform(streams_of[2], (NZ, NXI, NYI), jnp.float32) ** levels(streams_of[2], (NZ, NXI, NYI), ((1, 32), (2, 4)), -0.2, 0.2)), 0.02, 0.15),
        "skin_humidity": jnp.clip(0.6 + 0.39999998 * jax.random.uniform(streams_of[3], (DEPTH, HS, PER), jnp.float32) ** levels(streams_of[3], (DEPTH, HS, PER), ((1, 4), (2, 32)), -0.2, 0.2), 0.6, 1.0),
        "skin_temp": jnp.clip(2.0 * jax.random.uniform(streams_of[4], (DEPTH, HS, PER), jnp.float32) ** levels(streams_of[4], (DEPTH, HS, PER), ((1, 4), (2, 32)), -0.2, 0.2), 0.0, 2.0),
        "skin_degree": jnp.clip(0.05 + 0.55 * jax.random.uniform(streams_of[5], (DEPTH, HS, PER), jnp.float32) ** levels(streams_of[5], (DEPTH, HS, PER), ((1, 4), (2, 32)), -0.2, 0.2), 0.05, 0.6),
        "ambient": jnp.clip(0.4 + 0.4 * jax.random.uniform(streams_of[6], (HS, PER), jnp.float32) ** levels(streams_of[6], (HS, PER), ((0, 4), (1, 32)), -0.2, 0.2), 0.4, 0.8),
        "colmap": draw_colmap(jax.random.fold_in(streams_of[8], 71), 0),
    }


def arrhenius(field, energy):
    return jnp.exp(energy * (1.0 / 293.15 - 1.0 / (293.15 + 10.0 * field)))


def neighbour_views(padded):
    return [padded[2:, 1:-1, 1:-1], padded[:-2, 1:-1, 1:-1], padded[1:-1, 2:, 1:-1],
            padded[1:-1, :-2, 1:-1], padded[1:-1, 1:-1, 2:], padded[1:-1, 1:-1, :-2]]


def interior_update(padded, thermal, degree, affinity):
    views = neighbour_views(padded)
    laplace = views[0] + views[1] + views[2] + views[3] + views[4] + views[5] - 6.0 * thermal
    hydration = affinity * (0.85 - degree) * arrhenius(thermal, 4000.0)
    return thermal + 0.15 * laplace + 4.0 * hydration, degree + hydration


def skin_step(hum_pad, temp_pad, degree, bound_temp, ambient):
    inner_hum = jnp.ones((1,) + hum_pad.shape[1:], jnp.float32)
    outer_hum = jnp.pad(ambient, 1)[None]
    hum_full = jnp.concatenate([inner_hum, hum_pad, outer_hum], axis=0)
    temp_full = jnp.concatenate([jnp.pad(bound_temp, 1)[None], temp_pad, temp_pad[-1:]], axis=0)
    diffusion = 0.07 * (0.05 + 0.95 / (1.0 + ((1.0 - hum_full) / 0.25) ** 8)) * arrhenius(temp_full, 2700.0)
    hum_mid = hum_full[1:-1, 1:-1, 1:-1]
    temp_mid = temp_full[1:-1, 1:-1, 1:-1]
    diff_mid = diffusion[1:-1, 1:-1, 1:-1]
    moisture = jnp.zeros_like(hum_mid)
    conduction = jnp.zeros_like(temp_mid)
    for hum_view, temp_view, diff_view in zip(neighbour_views(hum_full), neighbour_views(temp_full), neighbour_views(diffusion)):
        moisture = moisture + 0.5 * (diff_mid + diff_view) * (hum_view - hum_mid)
        conduction = conduction + (temp_view - temp_mid)
    hydration = 0.08 * (0.85 - degree) * arrhenius(temp_mid, 4000.0) / (1.0 + (7.5 - 7.5 * hum_mid) ** 4)
    evaporation = 0.5 * (diff_mid[-1] + diffusion[-1, 1:-1, 1:-1]) * (hum_mid[-1] - ambient)
    hum_new = hum_mid + moisture - 0.3 * hydration
    temp_new = temp_mid + 0.15 * conduction + 4.0 * hydration
    temp_new = temp_new.at[-1].add(-2.0 * evaporation)
    inflow = 0.15 * (bound_temp - temp_mid[0])
    return hum_new, temp_new, degree + hydration, inflow


def pad_skin(field):
    field = jnp.pad(field, ((0, 0), (1, 1), (0, 0)), mode="edge")
    return jnp.pad(field, ((0, 0), (0, 0), (1, 1)), mode="wrap")


def reference(int_temp, int_degree, int_affinity, skin_humidity, skin_temp, skin_degree, ambient, colmap):
    thermal, degree = int_temp, int_degree
    for stepno in range(INT_STEPS):
        padded = jnp.pad(thermal, 1, mode="edge")
        thermal, degree = interior_update(padded, thermal, degree, int_affinity)
    coarse = thermal.reshape(NZ, NXI // CB, CB, NYI // CB, CB).mean(axis=(2, 4))
    coarse = coarse.reshape(NZ, N_BLK, IX // CB, N_HA, IY // CB).transpose(0, 1, 3, 2, 4).reshape(NZ, NCOL)
    bound = jnp.repeat(jnp.take(coarse, colmap, axis=1), HS // NZ, axis=0)
    hum, temp, sdeg = skin_humidity, skin_temp, skin_degree
    total = jnp.zeros((HS, PER), jnp.float32)
    for substep in range(SUB):
        hum, temp, sdeg, inflow = skin_step(pad_skin(hum), pad_skin(temp), sdeg, bound, ambient)
        total = total + inflow
    per_layer = total.reshape(NZ, HS // NZ, PER).sum(axis=1)
    uptake = jnp.zeros((NZ, NCOL), jnp.float32).at[:, colmap].add(per_layer)
    cells = uptake.reshape(NZ, N_BLK, N_HA, IX // CB, IY // CB).transpose(0, 1, 3, 2, 4).reshape(NZ, NXI // CB, NYI // CB)
    cells = jnp.repeat(jnp.repeat(cells, CB, axis=1), CB, axis=2)
    thermal_out = thermal - 0.5 * cells / (CB * CB)
    return thermal_out, degree, hum, temp
```

```python
import math

import jax
import jax.numpy as jnp
from jax import lax
from jax.experimental import pallas as pl
from jax.experimental.pallas import tpu as pltpu
from jax.sharding import PartitionSpec as P

F32 = jnp.float32
BF16 = jnp.bfloat16
MESH = pl.DeviceIdType.MESH

NZ, IX, IY = 32, 32, 256
DEPTH, ROWS, ARCS = 16, 64, 256
NB, NH = 32, 4
XC, RC = IX // 8, ROWS // 8
LN = 128

C27 = 2700.0 / 293.15 * math.log2(math.e)
C40 = 4000.0 / 293.15 * math.log2(math.e)

BULK = (0, 1, 2, 3)
WEDGE = (None, 4, 5, 6)
N_EX = 7


def rcp(x):
    r = pl.reciprocal(x, approx=True)
    return r * (2.0 - x * r)


def half_diff(h, t):
    s = 1.0 - h
    s2 = s * s
    s4 = s2 * s2
    q = t * rcp(29.315 + t)
    return (0.00175 + 0.03325 * rcp(1.0 + 65536.0 * (s4 * s4))) * jnp.exp2(C27 * q)


def rates(h, t):
    s = 1.0 - h
    s2 = s * s
    s4 = s2 * s2
    q = t * rcp(29.315 + t)
    d = (0.00175 + 0.03325 * rcp(1.0 + 65536.0 * (s4 * s4))) * jnp.exp2(C27 * q)
    g = 0.08 * rcp(1.0 + 3164.0625 * s4) * jnp.exp2(C40 * q)
    return d, g


def split3(a):
    a1 = a.astype(BF16).astype(F32)
    r1 = a - a1
    a2 = r1.astype(BF16).astype(F32)
    a3 = r1 - a2
    return jnp.concatenate([a1, a2, a3], axis=0).astype(BF16)


def pick(a, b, transpose_b=False):
    rows = a.shape[0]
    dims = (((1,), (1 if transpose_b else 0,)), ((), ()))
    out = lax.dot_general(split3(a), b, dims, preferred_element_type=F32)
    return out[:rows] + out[rows : 2 * rows] + out[2 * rows :]


def body(
    temp_in, deg_in, aff_in, hum_in, stemp_in, sdeg_in, amb_ref, col_ref,
    temp_out, deg_out, hum_out, stemp_out,
    th0, th1, al, af, hb0, hb1, tb0, tb1, db0, db1, gb, ab,
    cs, cr, rs, rr, ph, pd, dr, ics, icr, irs, irr,
    qs, qr, oh, o2, csum, csend, abuf, ws, rbuf, bnd, ub, vs, vr, ss, ubuf, ge,
    in_sem, out_sem, hs_send, hs_recv, q_send, q_recv, x1_send, x1_recv,
    x2_send, x2_recv, u2_send, u2_recv, u1_send, u1_recv,
):
    b = lax.axis_index("blk")
    ha = lax.axis_index("ha")
    lane = lax.broadcasted_iota(jnp.int32, (8, LN), 1)
    first = lane == 0
    final = lane == LN - 1
    lo, hi = slice(0, LN), slice(LN, 2 * LN)

    layers = pl.ds(1, NZ)
    slabs = pl.ds(1, DEPTH)
    xin = pl.ds(8, IX)
    rin = pl.ds(8, ROWS)
    loads = [
        pltpu.make_async_copy(src, dst, in_sem.at[i])
        for i, (src, dst) in enumerate(
            [
                (temp_in, th0.at[layers, xin, :]),
                (hum_in, hb0.at[slabs, rin, :]),
                (stemp_in, tb0.at[slabs, rin, :]),
                (aff_in, af),
                (deg_in, al),
                (sdeg_in, ab),
            ]
        )
    ]
    for copy in loads:
        copy.start()

    barrier = pltpu.get_barrier_semaphore()

    def greet(k, c):
        pl.semaphore_signal(barrier, inc=1, device_id=(lax.rem(b + k, NB), ha), device_id_type=MESH)
        return c

    lax.fori_loop(1, NB, greet, 0)
    for k in range(1, NH):
        pl.semaphore_signal(barrier, inc=1, device_id=(b, lax.rem(ha + k, NH)), device_id_type=MESH)

    col = col_ref[...]
    owner = col >> 7
    colf = jnp.broadcast_to(owner.astype(F32), (ARCS, ARCS))
    owner_down = colf.T
    q_i = lax.broadcasted_iota(jnp.int32, (ARCS, ARCS), 0)
    p_i = lax.broadcasted_iota(jnp.int32, (ARCS, ARCS), 1)
    earlier = jnp.where((owner_down == colf) & (q_i < p_i), 1.0, 0.0)
    rank = jnp.sum(earlier, axis=0, keepdims=True).astype(jnp.int32)
    ob = col >> 9
    pos = (ob >> 3) * LN + (((ob + b) & 7) << 4) + ((owner & 3) << 2) + rank
    posf = pos.astype(F32)
    pos_down = jnp.broadcast_to(posf, (LN, ARCS)).T
    val_down = jnp.broadcast_to((col & 511).astype(F32) + 1.0, (LN, ARCS)).T
    lanes_a = lax.broadcasted_iota(jnp.int32, (ARCS, LN), 1).astype(F32)
    for t in range(4):
        hit = jnp.where(pos_down == lanes_a + float(t * LN), val_down, 0.0)
        qs[t] = jnp.broadcast_to(jnp.sum(hit, axis=0, keepdims=True) - 1.0, (8, LN))
    slot_i = lax.broadcasted_iota(jnp.int32, (4 * LN, ARCS), 0).astype(F32)
    o2[...] = jnp.where(slot_i == posf, 1.0, 0.0).astype(BF16)

    zero = jnp.zeros((8, LN), F32)

    def clear(e, c):
        for side in range(2):
            for r in range(RC):
                cs[e, side, 8 * r : 8 * r + 8, :] = zero
            for f in range(2):
                rs[e, side, f] = jnp.zeros((DEPTH, ARCS), F32)
        return c

    lax.fori_loop(0, N_EX, clear, 0)
    for e in range(2):
        for side in range(2):
            ics[e, side] = jnp.zeros((IX, LN), F32)

    pl.semaphore_wait(barrier, NB - 1 + NH - 1)

    def to_blk(src, dst, send, recv):
        def go(k, c):
            to = lax.rem(b + k, NB)
            pltpu.make_async_remote_copy(
                src_ref=src.at[to // 8], dst_ref=dst.at[b], send_sem=send.at[to],
                recv_sem=recv.at[b], device_id=(to, ha), device_id_type=MESH,
            ).start()
            return c

        lax.fori_loop(1, NB, go, 0)

    def from_blk(src, dst, send, recv):
        def go(k, c):
            other = lax.rem(b + k, NB)
            copy = pltpu.make_async_remote_copy(
                src_ref=src.at[other // 8], dst_ref=dst.at[other], send_sem=send.at[other],
                recv_sem=recv.at[other], device_id=(other, ha), device_id_type=MESH,
            )
            copy.wait_send()
            copy.wait_recv()
            return c

        lax.fori_loop(1, NB, go, 0)
        dst[b] = src[b // 8]

    def combine(buf):
        tiles = []
        for t in range(4):
            acc = zero
            for j in range(8):
                acc = jnp.where((lane >> 4) == ((b + j) & 7), buf[t * 8 + j], acc)
            tiles.append(acc)
        return tiles

    def to_ha(src, dst, send, recv):
        for k in range(1, NH):
            to = lax.rem(ha + k, NH)
            pltpu.make_async_remote_copy(
                src_ref=src.at[to], dst_ref=dst.at[ha], send_sem=send.at[to],
                recv_sem=recv.at[ha], device_id=(b, to), device_id_type=MESH,
            ).start()

    def from_ha(src, dst, send, recv):
        for k in range(1, NH):
            other = lax.rem(ha + k, NH)
            copy = pltpu.make_async_remote_copy(
                src_ref=src.at[other], dst_ref=dst.at[other], send_sem=send.at[other],
                recv_sem=recv.at[other], device_id=(b, other), device_id_type=MESH,
            )
            copy.wait_send()
            copy.wait_recv()
        dst[ha] = src[ha]

    b_dn, b_up = lax.rem(b + NB - 1, NB), lax.rem(b + 1, NB)
    h_dn, h_up = lax.rem(ha + NH - 1, NH), lax.rem(ha + 1, NH)

    def halo(e, src_blk, dst_blk, src_ha, dst_ha):
        return [
            pltpu.make_async_remote_copy(
                src_ref=src.at[side], dst_ref=dst.at[1 - side],
                send_sem=hs_send.at[e, i], recv_sem=hs_recv.at[e, i],
                device_id=dev, device_id_type=MESH,
            )
            for i, (src, dst, side, dev) in enumerate(
                [
                    (src_blk, dst_blk, 0, (b_dn, ha)),
                    (src_blk, dst_blk, 1, (b_up, ha)),
                    (src_ha, dst_ha, 0, (b, h_dn)),
                    (src_ha, dst_ha, 1, (b, h_up)),
                ]
            )
        ]

    def skin_halo(e):
        return halo(e, cs.at[e], cr.at[e], rs.at[e], rr.at[e])

    def int_halo(e):
        return halo(N_EX + e, irs.at[e], irr.at[e], ics.at[e], icr.at[e])

    def start(copies):
        for copy in copies:
            copy.start()

    def wait(copies):
        for copy in copies:
            copy.wait()

    sub = lax.broadcasted_iota(jnp.int32, (8, LN), 0)

    def put_row(ref, m, row, half):
        tile = pl.ds(pl.multiple_of(((m - 1) // 8) * 8, 8), 8)
        here = sub == lax.rem(m - 1, 8)
        ref[tile, half] = jnp.where(here, jnp.broadcast_to(row, (8, LN)), ref[tile, half])

    def int_pack(e, m, r, x0, x1):
        rows = slice(8 * r, 8 * r + 8)
        ics[e, 0, rows, :] = jnp.where(lane == m, pltpu.roll(x0, m, 1), ics[e, 0, rows, :])
        ics[e, 1, rows, :] = jnp.where(lane == m, pltpu.roll(x1, m + 1, 1), ics[e, 1, rows, :])
        for side, at, k in ((0, 0, 0), (1, XC - 1, 7)):
            if r == at:
                for x, half in ((x0, lo), (x1, hi)):
                    put_row(irs.at[e, side], m, x[k : k + 1], half)

    def int_place(e, th):
        @pl.when(b == 0)
        def _():
            irr[e, 0] = irs[e, 0]

        @pl.when(b == NB - 1)
        def _():
            irr[e, 1] = irs[e, 1]

        @pl.when(ha == 0)
        def _():
            icr[e, 0] = ics[e, 0]

        @pl.when(ha == NH - 1)
        def _():
            icr[e, 1] = ics[e, 1]

        def go(m, c):
            th[m, 7:8, :] = irr[e, 0, pl.ds(m - 1, 1), :]
            th[m, 8 + IX : 9 + IX, :] = irr[e, 1, pl.ds(m - 1, 1), :]
            return c

        lax.fori_loop(1, NZ + 1, go, 0)
        th[0, 8 : 8 + IX, :] = th[1, 8 : 8 + IX, :]
        th[NZ + 1, 8 : 8 + IX, :] = th[NZ, 8 : 8 + IX, :]

    def sides(x0, x1, gl, gr):
        a1, b1 = pltpu.roll(x0, 1, 1), pltpu.roll(x1, 1, 1)
        a2, b2 = pltpu.roll(x0, LN - 1, 1), pltpu.roll(x1, LN - 1, 1)
        left = (jnp.where(first, gl, a1), jnp.where(first, a1, b1))
        right = (jnp.where(final, b2, a2), jnp.where(final, gr, b2))
        return left, right

    def int_step(e, src, dst, last):
        def go(m, c):
            for r in range(XC):
                rows = slice(8 * r, 8 * r + 8)
                x = [src[m, 8 + 8 * r : 16 + 8 * r, half] for half in (lo, hi)]
                gl = pltpu.roll(icr[e, 0, rows, :], LN - m, 1)
                gr = pltpu.roll(icr[e, 1, rows, :], LN - 1 - m, 1)
                left, right = sides(x[0], x[1], gl, gr)
                new = []
                for i, half in enumerate((lo, hi)):
                    t = x[i]
                    total = (
                        left[i] + right[i]
                        + src[m, 7 + 8 * r : 15 + 8 * r, half]
                        + src[m, 9 + 8 * r : 17 + 8 * r, half]
                        + src[m - 1, 8 + 8 * r : 16 + 8 * r, half]
                        + src[m + 1, 8 + 8 * r : 16 + 8 * r, half]
                    )
                    alpha = al[m - 1, rows, half]
                    rate = jnp.exp2(C40 * (t * rcp(29.315 + t)))
                    rise = af[m - 1, rows, half] * (0.85 - alpha) * rate
                    out = t + 0.15 * (total - 6.0 * t) + 4.0 * rise
                    al[m - 1, rows, half] = alpha + rise
                    dst[m, 8 + 8 * r : 16 + 8 * r, half] = out
                    new.append(out)
                    if last:
                        put_row(csum.at[r], m, jnp.sum(out, axis=0, keepdims=True), half)
                if not last:
                    int_pack(1, m, r, new[0], new[1])
            return c

        lax.fori_loop(1, NZ + 1, go, 0)

    states = ((hb0, tb0, db0), (hb1, tb1, db1))

    def skin_pack(e, m, r, h, t):
        rows = slice(8 * r, 8 * r + 8)
        for side in range(2):
            sh = m + side
            old = cs[e, side, rows, :]
            new = jnp.where(lane == m, pltpu.roll(h[side], sh, 1), old)
            cs[e, side, rows, :] = jnp.where(lane == m + 64, pltpu.roll(t[side], sh + 64, 1), new)
        for side, at, k in ((0, 0, 0), (1, RC - 1, 7)):
            if r == at:
                for f, x in enumerate((h, t)):
                    for i, half in enumerate((lo, hi)):
                        put_row(rs.at[e, side, f], m, x[i][k : k + 1], half)

    def skin_air(buf):
        H, T, D = buf
        for r in range(RC):
            rows = slice(8 + 8 * r, 16 + 8 * r)
            t = T[DEPTH, rows, :]
            T[DEPTH + 1, rows, :] = t
            D[DEPTH + 1, rows, :] = half_diff(H[DEPTH + 1, rows, :], t)

    def skin_first():
        H, T, D = states[0]
        for r in range(RC):
            rows = slice(8 + 8 * r, 16 + 8 * r)
            for buf in (hb0, hb1):
                buf[0, rows, :] = jnp.ones((8, ARCS), F32)
                buf[DEPTH + 1, rows, :] = amb_ref[8 * r : 8 * r + 8, :]

        def go(m, c):
            for r in range(RC):
                h = [H[m, 8 + 8 * r : 16 + 8 * r, half] for half in (lo, hi)]
                t = [T[m, 8 + 8 * r : 16 + 8 * r, half] for half in (lo, hi)]
                for i, half in enumerate((lo, hi)):
                    d, g = rates(h[i], t[i])
                    D[m, 8 + 8 * r : 16 + 8 * r, half] = d
                    gb[m - 1, 8 * r : 8 * r + 8, half] = g
                skin_pack(0, m, r, h, t)
            return c

        lax.fori_loop(1, DEPTH + 1, go, 0)
        skin_air(states[0])

    def skin_place(k, e, begin, end, wedge):
        H, T, D = states[k % 2]

        @pl.when(ha == 0)
        def _():
            rr[e, 0] = rs[e, 0]

        @pl.when(ha == NH - 1)
        def _():
            rr[e, 1] = rs[e, 1]

        for side in range(2):
            dr[side] = half_diff(rr[e, side, 0], rr[e, side, 1])
            for r in range(RC):
                rows = slice(8 * r, 8 * r + 8)
                x = cr[e, side, rows, :]
                d = half_diff(x, pltpu.roll(x, 64, 1))
                if wedge:
                    new = (lane & 63) <= k
                    x = jnp.where(new, x, ph[k, side, rows, :])
                    d = jnp.where(new, d, pd[k, side, rows, :])
                ph[k, side, rows, :] = x
                pd[k, side, rows, :] = d

        def go(m, c):
            for side, row in ((0, 7), (1, 8 + ROWS)):
                H[m, row : row + 1, :] = rr[e, side, 0, pl.ds(m - 1, 1), :]
                T[m, row : row + 1, :] = rr[e, side, 1, pl.ds(m - 1, 1), :]
                D[m, row : row + 1, :] = dr[side, pl.ds(m - 1, 1), :]
            return c

        lax.fori_loop(begin + 1, end + 1, go, 0)

    def skin_step(k, begin, end, e):
        H, T, D = states[k % 2]
        Hn, Tn, Dn = states[(k + 1) % 2]

        def go(m, c):
            air = jnp.where(m == DEPTH, 2.0, 0.0).astype(F32)
            for r in range(RC):
                rows = slice(8 * r, 8 * r + 8)
                mid = slice(8 + 8 * r, 16 + 8 * r)
                top = slice(7 + 8 * r, 15 + 8 * r)
                bot = slice(9 + 8 * r, 17 + 8 * r)
                h = [H[m, mid, half] for half in (lo, hi)]
                t = [T[m, mid, half] for half in (lo, hi)]
                d = [D[m, mid, half] for half in (lo, hi)]
                pl_, pr_ = ph[k, 0, rows, :], ph[k, 1, rows, :]
                hl, hr = sides(h[0], h[1], pltpu.roll(pl_, LN - m, 1), pltpu.roll(pr_, LN - 1 - m, 1))
                tl, tr = sides(t[0], t[1], pltpu.roll(pl_, 64 - m, 1), pltpu.roll(pr_, 63 - m, 1))
                dl, dr_ = sides(
                    d[0], d[1],
                    pltpu.roll(pd[k, 0, rows, :], LN - m, 1),
                    pltpu.roll(pd[k, 1, rows, :], LN - 1 - m, 1),
                )
                hn, tn = [], []
                for i, half in enumerate((lo, hi)):
                    hc, tc, dc = h[i], t[i], d[i]
                    out = (dc + D[m + 1, mid, half]) * (H[m + 1, mid, half] - hc)
                    moist = (
                        out
                        + (dc + D[m - 1, mid, half]) * (H[m - 1, mid, half] - hc)
                        + (dc + D[m, top, half]) * (H[m, top, half] - hc)
                        + (dc + D[m, bot, half]) * (H[m, bot, half] - hc)
                        + (dc + dl[i]) * (hl[i] - hc)
                        + (dc + dr_[i]) * (hr[i] - hc)
                    )
                    total = (
                        T[m + 1, mid, half] + T[m - 1, mid, half]
                        + T[m, top, half] + T[m, bot, half] + tl[i] + tr[i]
                    )
                    a = ab[m - 1, rows, half]
                    hyd = gb[m - 1, rows, half] * (0.85 - a)
                    h1 = hc + moist - 0.3 * hyd
                    t1 = tc + 0.15 * (total - 6.0 * tc) + 4.0 * hyd + air * out
                    Hn[m, mid, half] = h1
                    Tn[m, mid, half] = t1
                    if k < 3:
                        ab[m - 1, rows, half] = a + hyd
                        d1, g1 = rates(h1, t1)
                        Dn[m, mid, half] = d1
                        gb[m - 1, rows, half] = g1
                    hn.append(h1)
                    tn.append(t1)
                if k < 3:
                    skin_pack(e, m, r, hn, tn)
            return c

        lax.fori_loop(begin + 1, end + 1, go, 0)
        if end == DEPTH and k < 3:
            skin_air(states[(k + 1) % 2])

    def inflow(k):
        T = states[k % 2][1]
        for r in range(RC):
            rows = slice(8 + 8 * r, 16 + 8 * r)
            gain = jnp.sum(T[0, rows, :] - T[1, rows, :], axis=0, keepdims=True)
            if k:
                gain = gain + ub[r : r + 1, :]
            ub[r : r + 1, :] = gain

    to_blk(qs, qr, q_send, q_recv)
    loads[0].wait()

    def pack0(m, c):
        for r in range(XC):
            x = [th0[m, 8 + 8 * r : 16 + 8 * r, half] for half in (lo, hi)]
            int_pack(0, m, r, x[0], x[1])
        return c

    lax.fori_loop(1, NZ + 1, pack0, 0)
    ex_i0 = int_halo(0)
    start(ex_i0)
    loads[1].wait()
    loads[2].wait()
    skin_first()
    ex_s0 = skin_halo(0)
    start(ex_s0)

    loads[3].wait()
    loads[4].wait()
    wait(ex_i0)
    int_place(0, th0)
    int_step(0, th0, th1, False)
    ex_i1 = int_halo(1)
    start(ex_i1)

    loads[5].wait()
    wait(ex_s0)
    skin_place(0, 0, 0, DEPTH, False)
    skin_step(0, 1, DEPTH, BULK[1])
    ex_b1 = skin_halo(BULK[1])
    start(ex_b1)

    wait(ex_i1)
    int_place(1, th1)
    int_step(1, th1, th0, True)
    store_deg = pltpu.make_async_copy(al, deg_out, out_sem.at[0])
    store_deg.start()
    y_i = lax.broadcasted_iota(jnp.int32, (IY, LN), 0)
    c_i = lax.broadcasted_iota(jnp.int32, (IY, LN), 1)

    def mean_matrix(i):
        return jnp.where(((c_i >> 5) == i) & ((c_i & 31) == (y_i >> 3)), 1.0 / 64.0, 0.0).astype(BF16)

    coarse = jnp.zeros((NZ, LN), F32)
    for i in range(XC):
        coarse = coarse + pick(csum[i], mean_matrix(i))
    for i in range(NH):
        csend[i] = coarse[8 * i : 8 * i + 8]
    to_ha(csend, abuf, x1_send, x1_recv)

    from_blk(qs, qr, q_send, q_recv)
    slots = combine(qr)
    for t in range(4):
        key = jnp.broadcast_to(slots[t][0:1], (4 * LN, LN))
        row = lax.broadcasted_iota(jnp.int32, (4 * LN, LN), 0).astype(F32)
        oh[:, t * LN : (t + 1) * LN] = jnp.where(row == key, 1.0, 0.0).astype(BF16)

    wait(ex_b1)
    skin_place(1, BULK[1], 1, DEPTH, False)

    from_ha(csend, abuf, x1_send, x1_recv)
    wide = pick(jnp.concatenate([abuf[i] for i in range(NH)], axis=1), oh[...])
    for t in range(4):
        ws[t] = wide[:, t * LN : (t + 1) * LN]
    to_blk(ws, rbuf, x2_send, x2_recv)

    skin_step(1, 2, DEPTH, BULK[2])
    ex_b2 = skin_halo(BULK[2])
    start(ex_b2)

    from_blk(ws, rbuf, x2_send, x2_recv)
    bound = pick(jnp.concatenate(combine(rbuf), axis=1), o2[...])
    bnd[...] = bound
    bnd_d = half_diff(jnp.ones((8, ARCS), F32), bound)
    for r in range(RC):
        rows = slice(8 + 8 * r, 16 + 8 * r)
        for _, T, D in states:
            T[0, rows, :] = jnp.broadcast_to(bound[r : r + 1], (8, ARCS))
            D[0, rows, :] = jnp.broadcast_to(bnd_d[r : r + 1], (8, ARCS))

    inflow(0)
    skin_step(0, 0, 1, WEDGE[1])
    ex_w1 = skin_halo(WEDGE[1])
    start(ex_w1)
    inflow(1)

    wait(ex_b2)
    skin_place(2, BULK[2], 2, DEPTH, False)
    skin_step(2, 3, DEPTH, BULK[3])
    ex_b3 = skin_halo(BULK[3])
    start(ex_b3)

    wait(ex_w1)
    skin_place(1, WEDGE[1], 0, 1, True)
    skin_step(1, 0, 2, WEDGE[2])
    ex_w2 = skin_halo(WEDGE[2])
    start(ex_w2)
    inflow(2)

    wait(ex_b3)
    skin_place(3, BULK[3], 3, DEPTH, False)
    skin_step(3, 10, DEPTH, None)

    wait(ex_w2)
    skin_place(2, WEDGE[2], 0, 2, True)
    skin_step(2, 0, 3, WEDGE[3])
    ex_w3 = skin_halo(WEDGE[3])
    start(ex_w3)
    inflow(3)
    heat = pick(0.15 * ub[...], o2[...], transpose_b=True)
    for t in range(4):
        vs[t] = heat[:, t * LN : (t + 1) * LN]
    to_blk(vs, vr, u2_send, u2_recv)

    skin_step(3, 4, 10, None)
    wait(ex_w3)
    skin_place(3, WEDGE[3], 0, 3, True)

    from_blk(vs, vr, u2_send, u2_recv)
    summed = pick(jnp.concatenate(combine(vr), axis=1), oh[...], transpose_b=True)
    for i in range(NH):
        ss[i] = summed[:, i * LN : (i + 1) * LN]
    to_ha(ss, ubuf, u1_send, u1_recv)

    skin_step(3, 0, 4, None)
    store_h = pltpu.make_async_copy(hb0.at[slabs, rin, :], hum_out, out_sem.at[1])
    store_t = pltpu.make_async_copy(tb0.at[slabs, rin, :], stemp_out, out_sem.at[2])
    store_h.start()
    store_t.start()

    from_ha(ss, ubuf, u1_send, u1_recv)
    uptake = jnp.concatenate([ubuf[i] for i in range(NH)], axis=0)
    for i in range(XC):
        ge[i] = 0.5 * pick(uptake, mean_matrix(i), transpose_b=True)

    def finish(m, c):
        for r in range(XC):
            mid = slice(8 + 8 * r, 16 + 8 * r)
            th0[m, mid, :] = th0[m, mid, :] - ge[r, pl.ds(m - 1, 1), :]
        return c

    lax.fori_loop(1, NZ + 1, finish, 0)
    store_th = pltpu.make_async_copy(th0.at[layers, xin, :], temp_out, out_sem.at[3])
    store_th.start()
    for copy in (store_deg, store_h, store_t, store_th):
        copy.wait()


def on_device(int_temp, int_degree, int_affinity, hum, stemp, sdeg, ambient, colmap):
    vmem = pltpu.VMEM
    sem = pltpu.SemaphoreType.DMA
    skin_buf = vmem((DEPTH + 2, ROWS + 16, ARCS), F32)
    int_buf = vmem((NZ + 2, IX + 16, IY), F32)
    anywhere = pl.BlockSpec(memory_space=pl.ANY)
    inside = pl.BlockSpec(memory_space=pltpu.VMEM)
    interior = jax.ShapeDtypeStruct((NZ, IX, IY), F32)
    skin = jax.ShapeDtypeStruct((DEPTH, ROWS, ARCS), F32)
    msg = vmem((NB, 8, LN), F32)
    tiles = vmem((4, 8, LN), F32)
    return pl.pallas_call(
        body,
        out_shape=(interior, interior, skin, skin),
        in_specs=[anywhere] * 6 + [inside] * 2,
        out_specs=(anywhere,) * 4,
        scratch_shapes=[
            int_buf, int_buf, vmem((NZ, IX, IY), F32), vmem((NZ, IX, IY), F32),
            skin_buf, skin_buf, skin_buf, skin_buf, skin_buf, skin_buf,
            vmem((DEPTH, ROWS, ARCS), F32), vmem((DEPTH, ROWS, ARCS), F32),
            vmem((N_EX, 2, ROWS, LN), F32), vmem((N_EX, 2, ROWS, LN), F32),
            vmem((N_EX, 2, 2, DEPTH, ARCS), F32), vmem((N_EX, 2, 2, DEPTH, ARCS), F32),
            vmem((4, 2, ROWS, LN), F32), vmem((4, 2, ROWS, LN), F32),
            vmem((2, DEPTH, ARCS), F32),
            vmem((2, 2, IX, LN), F32), vmem((2, 2, IX, LN), F32),
            vmem((2, 2, NZ, IY), F32), vmem((2, 2, NZ, IY), F32),
            tiles, msg, vmem((4 * LN, 4 * LN), BF16), vmem((4 * LN, ARCS), BF16),
            vmem((XC, NZ, IY), F32), tiles, tiles, tiles, msg,
            vmem((8, ARCS), F32), vmem((8, ARCS), F32), tiles, msg, tiles, tiles,
            vmem((XC, NZ, IY), F32),
            sem((6,)), sem((4,)), sem((N_EX + 2, 4)), sem((N_EX + 2, 4)),
            sem((NB,)), sem((NB,)), sem((NH,)), sem((NH,)),
            sem((NB,)), sem((NB,)), sem((NB,)), sem((NB,)), sem((NH,)), sem((NH,)),
        ],
        compiler_params=pltpu.CompilerParams(
            collective_id=0, has_side_effects=True, vmem_limit_bytes=48 * 1024 * 1024
        ),
        name="pylon",
    )(int_temp, int_degree, int_affinity, hum, stemp, sdeg, ambient, colmap.reshape(1, ARCS))


def solution(mesh):
    plan = P(None, "blk", "ha")
    band = P(None, "ha", "blk")
    return jax.shard_map(
        on_device,
        mesh=mesh,
        in_specs=(plan, plan, plan, band, band, band, P("ha", "blk"), P("blk")),
        out_specs=(plan, plan, band, band),
        check_vma=False,
    )
```

```python
import math

import jax
import jax.numpy as jnp
from jax import lax
from jax.experimental import pallas as pl
from jax.experimental.pallas import tpu as pltpu
from jax.sharding import PartitionSpec as P

F32 = jnp.float32
BF16 = jnp.bfloat16
MESH = pl.DeviceIdType.MESH

NZ, IX, IY = 32, 32, 256
DEPTH, ROWS, ARCS = 16, 64, 256
NB, NH = 32, 4
XC, RC = IX // 8, ROWS // 8
LN = 128

C27 = 2700.0 / 293.15 * math.log2(math.e)
C40 = 4000.0 / 293.15 * math.log2(math.e)

BULK = (0, 1, 2, 3)
WEDGE = (None, 4, 5, 6)
N_EX = 7


def rcp(x):
    r = pl.reciprocal(x, approx=True)
    return r * (2.0 - x * r)


def half_diff(h, t):
    s = 1.0 - h
    s2 = s * s
    s4 = s2 * s2
    q = t * rcp(29.315 + t)
    return (0.00175 + 0.03325 * rcp(1.0 + 65536.0 * (s4 * s4))) * jnp.exp2(C27 * q)


def rates(h, t):
    s = 1.0 - h
    s2 = s * s
    s4 = s2 * s2
    q = t * rcp(29.315 + t)
    d = (0.00175 + 0.03325 * rcp(1.0 + 65536.0 * (s4 * s4))) * jnp.exp2(C27 * q)
    g = 0.08 * rcp(1.0 + 3164.0625 * s4) * jnp.exp2(C40 * q)
    return d, g


def split3(a):
    a1 = a.astype(BF16).astype(F32)
    r1 = a - a1
    a2 = r1.astype(BF16).astype(F32)
    a3 = r1 - a2
    return jnp.concatenate([a1, a2, a3], axis=0).astype(BF16)


def pick(a, b, transpose_b=False):
    rows = a.shape[0]
    dims = (((1,), (1 if transpose_b else 0,)), ((), ()))
    out = lax.dot_general(split3(a), b, dims, preferred_element_type=F32)
    return out[:rows] + out[rows : 2 * rows] + out[2 * rows :]


def both(whole, staged, sems, at, out=False):
    copies = []
    for i in range(2):
        half = slice(i * LN, (i + 1) * LN)
        if len(whole.shape) == 2:
            a, c = whole.at[:, half], staged.at[i]
        else:
            a, c = whole.at[:, :, half], staged.at[:, i]
        src, dst = (c, a) if out else (a, c)
        copies.append(pltpu.make_async_copy(src, dst, sems.at[2 * at + i]))
    return copies


def settle(*refs):
    loads, stores = [], []
    for i in range(4):
        half = refs[i].shape[0] // 2
        for k in range(2):
            part = pl.ds(k * half, half)
            n = 2 * i + k
            via = refs[8 + i].at[part]
            loads.append(pltpu.make_async_copy(refs[i].at[part], via, refs[12].at[n]))
            stores.append(pltpu.make_async_copy(via, refs[4 + i].at[part], refs[13].at[n]))
    for copy in loads:
        copy.start()
    for load, store in zip(loads, stores):
        load.wait()
        store.start()
    for copy in stores:
        copy.wait()


def body(
    temp_in, deg_in, aff_in, hum_in, stemp_in, sdeg_in, amb_in, col_in,
    temp_out, deg_out, hum_out, stemp_out,
    xt, xd, xa, xh, xs, xg, xm, col_ref,
    th0, th1, al, hb0, hb1, tb0, tb1, db0, db1, gb, ab,
    cs, cr, rs, rr, cg, dr, ics, icr, icg, irs, irr,
    qs, qr, oh, o2, csum, csend, abuf, ws, rbuf, ub, vs, vr, ss, ubuf, ge,
    in_sem, out_sem, hs_send, hs_recv, q_send, q_recv, x1_send, x1_recv,
    x2_send, x2_recv, u2_send, u2_recv, u1_send, u1_recv,
):
    b = lax.axis_index("blk")
    ha = lax.axis_index("ha")
    lane = lax.broadcasted_iota(jnp.int32, (8, LN), 1)
    first = lane == 0
    final = lane == LN - 1
    lo, hi = slice(0, LN), slice(LN, 2 * LN)

    halves = (lo, hi)

    col_load = pltpu.make_async_copy(col_in, col_ref, in_sem.at[14])
    col_load.start()
    loads = [
        both(src, dst, in_sem, i)
        for i, (src, dst) in enumerate(
            [
                (temp_in, xt), (hum_in, xh), (stemp_in, xs), (amb_in, xm),
                (aff_in, xa), (deg_in, xd), (sdeg_in, xg),
            ]
        )
    ]
    for copies in loads:
        for copy in copies:
            copy.start()

    barrier = pltpu.get_barrier_semaphore()

    def greet(k, c):
        pl.semaphore_signal(barrier, inc=1, device_id=(lax.rem(b + k, NB), ha), device_id_type=MESH)
        return c

    lax.fori_loop(1, NB, greet, 0)
    for k in range(1, NH):
        pl.semaphore_signal(barrier, inc=1, device_id=(b, lax.rem(ha + k, NH)), device_id_type=MESH)

    col_load.wait()

    col = col_ref[...]
    owner = col >> 7
    colf = jnp.broadcast_to(owner.astype(F32), (ARCS, ARCS))
    owner_down = colf.T
    q_i = lax.broadcasted_iota(jnp.int32, (ARCS, ARCS), 0)
    p_i = lax.broadcasted_iota(jnp.int32, (ARCS, ARCS), 1)
    earlier = jnp.where((owner_down == colf) & (q_i < p_i), 1.0, 0.0)
    rank = jnp.sum(earlier, axis=0, keepdims=True).astype(jnp.int32)
    ob = col >> 9
    pos = (ob >> 3) * LN + (((ob + b) & 7) << 4) + ((owner & 3) << 2) + rank
    posf = pos.astype(F32)
    pos_down = jnp.broadcast_to(posf, (LN, ARCS)).T
    val_down = jnp.broadcast_to((col & 511).astype(F32) + 1.0, (LN, ARCS)).T
    lanes_a = lax.broadcasted_iota(jnp.int32, (ARCS, LN), 1).astype(F32)
    for t in range(4):
        hit = jnp.where(pos_down == lanes_a + float(t * LN), val_down, 0.0)
        qs[t] = jnp.broadcast_to(jnp.sum(hit, axis=0, keepdims=True) - 1.0, (8, LN))
    slot_i = lax.broadcasted_iota(jnp.int32, (4 * LN, ARCS), 0).astype(F32)
    o2[...] = jnp.where(slot_i == posf, 1.0, 0.0).astype(BF16)

    zero = jnp.zeros((8, LN), F32)

    def clear(e, c):
        for side in range(2):
            for r in range(RC):
                cs[e, r] = zero
            for f in range(2):
                rs[e, side, f] = jnp.zeros((DEPTH, ARCS), F32)
        return c

    lax.fori_loop(0, N_EX, clear, 0)
    for e in range(2):
        for r in range(XC):
            ics[e, r] = zero

    pl.semaphore_wait(barrier, NB - 1 + NH - 1)

    def to_blk(src, dst, send, recv):
        def go(k, c):
            to = lax.rem(b + k, NB)
            pltpu.make_async_remote_copy(
                src_ref=src.at[to // 8], dst_ref=dst.at[b], send_sem=send.at[to],
                recv_sem=recv.at[b], device_id=(to, ha), device_id_type=MESH,
            ).start()
            return c

        lax.fori_loop(1, NB, go, 0)

    def from_blk(src, dst, send, recv):
        def go(k, c):
            other = lax.rem(b + k, NB)
            copy = pltpu.make_async_remote_copy(
                src_ref=src.at[other // 8], dst_ref=dst.at[other], send_sem=send.at[other],
                recv_sem=recv.at[other], device_id=(other, ha), device_id_type=MESH,
            )
            copy.wait_send()
            copy.wait_recv()
            return c

        lax.fori_loop(1, NB, go, 0)
        dst[b] = src[b // 8]

    def combine(buf):
        tiles = []
        for t in range(4):
            acc = zero
            for j in range(8):
                acc = jnp.where((lane >> 4) == ((b + j) & 7), buf[t * 8 + j], acc)
            tiles.append(acc)
        return tiles

    def to_ha(src, dst, send, recv):
        for k in range(1, NH):
            to = lax.rem(ha + k, NH)
            pltpu.make_async_remote_copy(
                src_ref=src.at[to], dst_ref=dst.at[ha], send_sem=send.at[to],
                recv_sem=recv.at[ha], device_id=(b, to), device_id_type=MESH,
            ).start()

    def from_ha(src, dst, send, recv):
        for k in range(1, NH):
            other = lax.rem(ha + k, NH)
            copy = pltpu.make_async_remote_copy(
                src_ref=src.at[other], dst_ref=dst.at[other], send_sem=send.at[other],
                recv_sem=recv.at[other], device_id=(b, other), device_id_type=MESH,
            )
            copy.wait_send()
            copy.wait_recv()
        dst[ha] = src[ha]

    b_dn, b_up = lax.rem(b + NB - 1, NB), lax.rem(b + 1, NB)
    h_dn, h_up = lax.rem(ha + NH - 1, NH), lax.rem(ha + 1, NH)

    def halo(e, src_blk, dst_blk, src_ha, dst_ha):
        return [
            pltpu.make_async_remote_copy(
                src_ref=src, dst_ref=dst, send_sem=hs_send.at[e, i],
                recv_sem=hs_recv.at[e, i], device_id=dev, device_id_type=MESH,
            )
            for i, (src, dst, dev) in enumerate(
                [
                    (src_blk[0], dst_blk.at[1], (b_dn, ha)),
                    (src_blk[1], dst_blk.at[0], (b_up, ha)),
                    (src_ha[0], dst_ha.at[1], (b, h_dn)),
                    (src_ha[1], dst_ha.at[0], (b, h_up)),
                ]
            )
        ]

    def skin_halo(e):
        cols, rows = cs.at[e], rs.at[e]
        return halo(e, (cols, cols), cr.at[e], (rows.at[0], rows.at[1]), rr.at[e])

    def int_halo(e):
        cols, rows = ics.at[e], irs.at[e]
        return halo(N_EX + e, (rows.at[0], rows.at[1]), irr.at[e], (cols, cols), icr.at[e])

    def sweep(go, begin, end):
        count = end - begin

        def two(i, c):
            go(begin + 2 * i)
            go(begin + 2 * i + 1)
            return c

        if count > 1:
            lax.fori_loop(0, count // 2, two, 0)
        if count % 2:
            go(end - 1)

    def start(copies):
        for copy in copies:
            copy.start()

    def wait(copies):
        for copy in copies:
            copy.wait()

    sub = lax.broadcasted_iota(jnp.int32, (8, LN), 0)

    def put_row(ref, m, row, half):
        tile = pl.ds(pl.multiple_of(((m - 1) // 8) * 8, 8), 8)
        here = sub == lax.rem(m - 1, 8)
        ref[tile, half] = jnp.where(here, jnp.broadcast_to(row, (8, LN)), ref[tile, half])

    pair = (lane + 1) >> 1
    odd = (lane & 1) == 1
    def shift_rows(x, ghost_row, up):
        ghost = jnp.broadcast_to(ghost_row, (8, LN))
        if up:
            return jnp.where(sub == 0, ghost, pltpu.roll(x, 1, 0))
        return jnp.where(sub == 7, ghost, pltpu.roll(x, 7, 0))

    def int_pack(e, m, r, x, mine):
        edge = pltpu.roll(jnp.where(final, x[1], x[0]), 2 * m, 1)
        ics[e, r] = jnp.where(mine, edge, ics[e, r])
        for side, at, k in ((0, 0, 0), (1, XC - 1, 7)):
            if r == at:
                for i, half in enumerate(halves):
                    put_row(irs.at[e, side], m, x[i][k : k + 1], half)

    def int_place(e, th):
        @pl.when(b == 0)
        def _():
            irr[e, 0] = irs[e, 0]

        @pl.when(b == NB - 1)
        def _():
            irr[e, 1] = irs[e, 1]

        at_low = jnp.full((8, LN), ha, jnp.int32) == 0
        at_high = jnp.full((8, LN), ha, jnp.int32) == NH - 1
        for r in range(XC):
            own = pltpu.roll(ics[e, r], LN - 1, 1)
            low = jnp.where(at_low, own, icr[e, 0, r])
            high = jnp.where(at_high, own, pltpu.roll(icr[e, 1, r], LN - 2, 1))
            icg[e, r] = jnp.where(odd, low, high)
            th[0, r] = th[1, r]
            th[NZ + 1, r] = th[NZ, r]

    def sides(x0, x1, ghost):
        a1, b1 = pltpu.roll(x0, 1, 1), pltpu.roll(x1, 1, 1)
        a2, b2 = pltpu.roll(x0, LN - 1, 1), pltpu.roll(x1, LN - 1, 1)
        left = (jnp.where(first, ghost, a1), jnp.where(first, a1, b1))
        right = (jnp.where(final, b2, a2), jnp.where(final, ghost, b2))
        return left, right

    def int_step(e, src, dst, last):
        def go(m):
            mine = pair == m
            sums = [0.0, 0.0]
            for r in range(XC):
                part = pl.ds(r, 8, stride=XC)
                x = [src[m, r, :, half] for half in halves]
                left, right = sides(x[0], x[1], pltpu.roll(icg[e, r], 129 - 2 * m, 1))
                new = []
                for i, half in enumerate(halves):
                    t = x[i]
                    if r == 0:
                        up = shift_rows(src[m, XC - 1, :, half], irr[e, 0, pl.ds(m - 1, 1), :][:, half], True)
                    else:
                        up = src[m, r - 1, :, half]
                    if r == XC - 1:
                        down = shift_rows(src[m, 0, :, half], irr[e, 1, pl.ds(m - 1, 1), :][:, half], False)
                    else:
                        down = src[m, r + 1, :, half]
                    total = (left[i] + right[i]) + (up + down) + (
                        src[m - 1, r, :, half] + src[m + 1, r, :, half]
                    )
                    alpha = al[m - 1, r, :, half] if last else xd[m - 1, i, part, :]
                    rate = jnp.exp2(C40 * (t * rcp(29.315 + t)))
                    rise = xa[m - 1, i, part, :] * (0.85 - alpha) * rate
                    out = t + 0.15 * (total - 6.0 * t) + 4.0 * rise
                    if last:
                        xd[m - 1, i, part, :] = alpha + rise
                        sums[i] = sums[i] + out
                    else:
                        al[m - 1, r, :, half] = alpha + rise
                    dst[m, r, :, half] = out
                    new.append(out)
                if not last:
                    int_pack(1, m, r, new, mine)
            if last:
                for i, half in enumerate(halves):
                    both = sums[i] + pltpu.roll(sums[i], 7, 0)
                    for r in range(XC):
                        put_row(csum.at[r], m, both[2 * r : 2 * r + 1], half)

        sweep(go, 1, NZ + 1)

    states = ((hb0, tb0, db0), (hb1, tb1, db1))

    def skin_pack(e, m, r, h, t, mine_h, mine_t):
        eh = pltpu.roll(jnp.where(final, h[1], h[0]), 2 * m, 1)
        et = pltpu.roll(jnp.where(final, t[1], t[0]), 2 * m + 40, 1)
        cs[e, r] = jnp.where(mine_t, et, jnp.where(mine_h, eh, cs[e, r]))
        for side, at, k in ((0, 0, 0), (1, RC - 1, 7)):
            if r == at:
                for f, x in enumerate((h, t)):
                    for i, half in enumerate(halves):
                        put_row(rs.at[e, side, f], m, x[i][k : k + 1], half)

    def skin_air(buf):
        H, T, D = buf
        for r in range(RC):
            t = T[DEPTH, r]
            T[DEPTH + 1, r] = t
            D[DEPTH + 1, r] = half_diff(H[DEPTH + 1, r], t)

    def skin_first():
        H, T, D = states[0]
        for r in range(RC):
            for i, half in enumerate(halves):
                air = xm[i, pl.ds(r, 8, stride=RC), :]
                for buf in (hb0, hb1):
                    buf[0, r, :, half] = jnp.ones((8, LN), F32)
                    buf[DEPTH + 1, r, :, half] = air

        def go(m, c):
            mine_h, mine_t = pair == m, pair == m + 20
            for r in range(RC):
                part = pl.ds(r, 8, stride=RC)
                h = [xh[m - 1, i, part, :] for i in range(2)]
                t = [xs[m - 1, i, part, :] for i in range(2)]
                for i, half in enumerate(halves):
                    d, g = rates(h[i], t[i])
                    H[m, r, :, half] = h[i]
                    T[m, r, :, half] = t[i]
                    D[m, r, :, half] = d
                    gb[m - 1, r, :, half] = g
                skin_pack(0, m, r, h, t, mine_h, mine_t)
            return c

        lax.fori_loop(1, DEPTH + 1, go, 0)
        skin_air(states[0])

    def skin_place(k, e, wedge):
        @pl.when(ha == 0)
        def _():
            rr[e, 0] = rs[e, 0]

        @pl.when(ha == NH - 1)
        def _():
            rr[e, 1] = rs[e, 1]

        if wedge:
            here = lax.broadcasted_iota(jnp.int32, (DEPTH, ARCS), 0) >= k
            for side in range(2):
                for f in range(2):
                    rr[e, side, f] = jnp.where(here, rr[BULK[k], side, f], rr[e, side, f])
        for side in range(2):
            dr[e, side] = half_diff(rr[e, side, 0], rr[e, side, 1])
        field = jnp.where(lane >= 80, lane - 80, jnp.where(lane >= 40, lane - 40, lane))
        fresh = (field >> 1) < k
        for r in range(RC):
            x = jnp.where(odd, cr[e, 0, r], pltpu.roll(cr[e, 1, r], LN - 2, 1))
            d = half_diff(x, pltpu.roll(x, LN - 40, 1))
            x = jnp.where(lane >= 80, pltpu.roll(d, 80, 1), x)
            cg[k, r] = jnp.where(fresh, x, cg[k, r]) if wedge else x

    def skin_step(k, begin, end, e, e_in):
        H, T, D = states[k % 2]
        Hn, Tn, Dn = states[(k + 1) % 2]

        def go(m):
            mine_h, mine_t = pair == m, pair == m + 20
            air = jnp.where(m == DEPTH, 2.0, 0.0)
            row = pl.ds(m - 1, 1)
            flow = [0.0, 0.0]
            for r in range(RC):
                part = pl.ds(r, 8, stride=RC)
                ghosts = cg[k, r]
                h = [H[m, r, :, half] for half in halves]
                t = [T[m, r, :, half] for half in halves]
                d = [D[m, r, :, half] for half in halves]
                gh, gt, gd = (pltpu.roll(ghosts, at - 2 * m, 1) for at in (129, 89, 49))
                tl, tr = sides(t[0], t[1], gt)
                h0, h1 = pltpu.roll(h[0], LN - 1, 1), pltpu.roll(h[1], LN - 1, 1)
                d0, d1 = pltpu.roll(d[0], LN - 1, 1), pltpu.roll(d[1], LN - 1, 1)
                f0 = (d[0] + jnp.where(final, d1, d0)) * (jnp.where(final, h1, h0) - h[0])
                f1 = (d[1] + jnp.where(final, gd, d1)) * (jnp.where(final, gh, h1) - h[1])
                s0, s1 = pltpu.roll(f0, 1, 1), pltpu.roll(f1, 1, 1)
                across = (
                    f0 - jnp.where(first, (d[0] + gd) * (h[0] - gh), s0),
                    f1 - jnp.where(first, s0, s1),
                )
                hn, tn = [], []
                for i, half in enumerate(halves):
                    hc, tc, dc = h[i], t[i], d[i]
                    if r == 0:
                        hu, tu, du = (
                            shift_rows(x[m, RC - 1, :, half], g[row, :][:, half], True)
                            for x, g in ((H, rr.at[e_in, 0, 0]), (T, rr.at[e_in, 0, 1]), (D, dr.at[e_in, 0]))
                        )
                        flow[i] = (du + dc) * (hc - hu)
                    else:
                        tu = T[m, r - 1, :, half]
                    if r == RC - 1:
                        hd, td, dd = (
                            shift_rows(x[m, 0, :, half], g[row, :][:, half], False)
                            for x, g in ((H, rr.at[e_in, 1, 0]), (T, rr.at[e_in, 1, 1]), (D, dr.at[e_in, 1]))
                        )
                    else:
                        hd, td, dd = H[m, r + 1, :, half], T[m, r + 1, :, half], D[m, r + 1, :, half]
                    below = (dc + dd) * (hd - hc)
                    out = (dc + D[m + 1, r, :, half]) * (H[m + 1, r, :, half] - hc)
                    into = (dc + D[m - 1, r, :, half]) * (H[m - 1, r, :, half] - hc)
                    moist = (out + into) + (below - flow[i]) + across[i]
                    flow[i] = below
                    total = (T[m + 1, r, :, half] + T[m - 1, r, :, half]) + (tu + td) + (tl[i] + tr[i])
                    a = xg[m - 1, i, part, :] if k == 0 else ab[m - 1, r, :, half]
                    hyd = gb[m - 1, r, :, half] * (0.85 - a)
                    h1_ = hc + moist - 0.3 * hyd
                    t1_ = tc + 0.15 * (total - 6.0 * tc) + 4.0 * hyd + air * out
                    if k < 3:
                        Hn[m, r, :, half] = h1_
                        Tn[m, r, :, half] = t1_
                        ab[m - 1, r, :, half] = a + hyd
                        dn, gn = rates(h1_, t1_)
                        Dn[m, r, :, half] = dn
                        gb[m - 1, r, :, half] = gn
                    else:
                        xh[m - 1, i, part, :] = h1_
                        xs[m - 1, i, part, :] = t1_
                    hn.append(h1_)
                    tn.append(t1_)
                if k < 3:
                    skin_pack(e, m, r, hn, tn, mine_h, mine_t)

        sweep(go, begin + 1, end + 1)
        if end == DEPTH and k < 3:
            skin_air(states[(k + 1) % 2])

    def inflow(k):
        T = states[k % 2][1]
        gain = 0.0 if k == 0 else ub[...]
        for r in range(RC):
            gain = gain + (T[0, r] - T[1, r])
        ub[...] = gain

    wait(loads[0])

    def pack0(m, c):
        mine = pair == m
        for r in range(XC):
            x = [xt[m - 1, i, pl.ds(r, 8, stride=XC), :] for i in range(2)]
            for i, half in enumerate(halves):
                th0[m, r, :, half] = x[i]
            int_pack(0, m, r, x, mine)
        return c

    lax.fori_loop(1, NZ + 1, pack0, 0, unroll=2)
    ex_i0 = int_halo(0)
    start(ex_i0)
    to_blk(qs, qr, q_send, q_recv)
    for i in (1, 2, 3):
        wait(loads[i])
    skin_first()
    ex_s0 = skin_halo(0)
    start(ex_s0)

    wait(loads[4])
    wait(loads[5])
    wait(ex_i0)
    int_place(0, th0)
    int_step(0, th0, th1, False)
    ex_i1 = int_halo(1)
    start(ex_i1)

    wait(loads[6])
    wait(ex_s0)
    skin_place(0, 0, False)
    skin_step(0, 1, DEPTH, BULK[1], BULK[0])
    ex_b1 = skin_halo(BULK[1])
    start(ex_b1)

    wait(ex_i1)
    int_place(1, th1)
    int_step(1, th1, th0, True)
    store_deg = both(deg_out, xd, out_sem, 0, True)
    start(store_deg)
    y_i = lax.broadcasted_iota(jnp.int32, (IY, LN), 0)
    c_i = lax.broadcasted_iota(jnp.int32, (IY, LN), 1)

    def mean_matrix(i):
        return jnp.where(((c_i >> 5) == i) & ((c_i & 31) == (y_i >> 3)), 1.0 / 64.0, 0.0).astype(BF16)

    coarse = jnp.zeros((NZ, LN), F32)
    for i in range(XC):
        coarse = coarse + pick(csum[i], mean_matrix(i))
    for i in range(NH):
        csend[i] = coarse[8 * i : 8 * i + 8]
    to_ha(csend, abuf, x1_send, x1_recv)

    from_blk(qs, qr, q_send, q_recv)
    slots = combine(qr)
    for t in range(4):
        key = jnp.broadcast_to(slots[t][0:1], (4 * LN, LN))
        row = lax.broadcasted_iota(jnp.int32, (4 * LN, LN), 0).astype(F32)
        oh[:, t * LN : (t + 1) * LN] = jnp.where(row == key, 1.0, 0.0).astype(BF16)

    wait(ex_b1)
    skin_place(1, BULK[1], False)

    from_ha(csend, abuf, x1_send, x1_recv)
    wide = pick(jnp.concatenate([abuf[i] for i in range(NH)], axis=1), oh[...])
    for t in range(4):
        ws[t] = wide[:, t * LN : (t + 1) * LN]
    to_blk(ws, rbuf, x2_send, x2_recv)

    skin_step(1, 2, DEPTH, BULK[2], BULK[1])
    ex_b2 = skin_halo(BULK[2])
    start(ex_b2)

    from_blk(ws, rbuf, x2_send, x2_recv)
    bound = pick(jnp.concatenate(combine(rbuf), axis=1), o2[...])
    bound_d = half_diff(jnp.ones((8, ARCS), F32), bound)
    for r in range(RC):
        for _, T, D in states:
            T[0, r] = bound
            D[0, r] = bound_d

    inflow(0)
    skin_step(0, 0, 1, WEDGE[1], BULK[0])
    ex_w1 = skin_halo(WEDGE[1])
    start(ex_w1)
    inflow(1)

    wait(ex_b2)
    skin_place(2, BULK[2], False)
    skin_step(2, 3, DEPTH, BULK[3], BULK[2])
    ex_b3 = skin_halo(BULK[3])
    start(ex_b3)

    wait(ex_w1)
    skin_place(1, WEDGE[1], True)
    skin_step(1, 0, 2, WEDGE[2], WEDGE[1])
    ex_w2 = skin_halo(WEDGE[2])
    start(ex_w2)
    inflow(2)

    wait(ex_b3)
    skin_place(3, BULK[3], False)
    skin_step(3, 10, DEPTH, None, BULK[3])

    wait(ex_w2)
    skin_place(2, WEDGE[2], True)
    skin_step(2, 0, 3, WEDGE[3], WEDGE[2])
    ex_w3 = skin_halo(WEDGE[3])
    start(ex_w3)
    inflow(3)
    heat = pick(0.15 * ub[...], o2[...], transpose_b=True)
    for t in range(4):
        vs[t] = heat[:, t * LN : (t + 1) * LN]
    to_blk(vs, vr, u2_send, u2_recv)

    skin_step(3, 4, 10, None, BULK[3])
    wait(ex_w3)
    skin_place(3, WEDGE[3], True)

    from_blk(vs, vr, u2_send, u2_recv)
    summed = pick(jnp.concatenate(combine(vr), axis=1), oh[...], transpose_b=True)
    for i in range(NH):
        ss[i] = summed[:, i * LN : (i + 1) * LN]
    to_ha(ss, ubuf, u1_send, u1_recv)

    skin_step(3, 0, 4, None, WEDGE[3])
    store_h = both(hum_out, xh, out_sem, 1, True)
    store_t = both(stemp_out, xs, out_sem, 2, True)
    start(store_h)
    start(store_t)

    from_ha(ss, ubuf, u1_send, u1_recv)
    uptake = jnp.concatenate([ubuf[i] for i in range(NH)], axis=0)
    for i in range(XC):
        ge[i] = 0.5 * pick(uptake, mean_matrix(i), transpose_b=True)

    def finish(m, c):
        for i, half in enumerate(halves):
            cool = jnp.zeros((8, LN), F32)
            for g in range(XC):
                row = jnp.broadcast_to(ge[g, pl.ds(m - 1, 1), :][:, half], (8, LN))
                cool = jnp.where((sub >> 1) == g, row, cool)
            for r in range(XC):
                xt[m - 1, i, pl.ds(r, 8, stride=XC), :] = th0[m, r, :, half] - cool
        return c

    lax.fori_loop(1, NZ + 1, finish, 0, unroll=2)
    store_th = both(temp_out, xt, out_sem, 3, True)
    start(store_th)
    for copies in (store_deg, store_h, store_t, store_th):
        wait(copies)


def on_device(int_temp, int_degree, int_affinity, hum, stemp, sdeg, ambient, colmap):
    vmem = pltpu.VMEM
    sem = pltpu.SemaphoreType.DMA
    skin_buf = vmem((DEPTH + 2, RC, 8, ARCS), F32)
    int_buf = vmem((NZ + 2, XC, 8, IY), F32)
    int_stage = vmem((NZ, 2, IX, LN), F32)
    skin_stage = vmem((DEPTH, 2, ROWS, LN), F32)
    outside = pl.BlockSpec(memory_space=pltpu.HBM)
    interior = jax.ShapeDtypeStruct((NZ, IX, IY), F32)
    skin = jax.ShapeDtypeStruct((DEPTH, ROWS, ARCS), F32)
    outs = (interior, interior, skin, skin)
    msg = vmem((NB, 8, LN), F32)
    tiles = vmem((4, 8, LN), F32)
    results = pl.pallas_call(
        body,
        out_shape=outs,
        in_specs=[outside] * 8,
        out_specs=(outside,) * 4,
        scratch_shapes=[
            int_stage, int_stage, int_stage, skin_stage, skin_stage, skin_stage,
            vmem((2, ROWS, LN), F32), vmem((1, ARCS), jnp.int32),
            int_buf, int_buf, vmem((NZ, XC, 8, IY), F32),
            skin_buf, skin_buf, skin_buf, skin_buf, skin_buf, skin_buf,
            vmem((DEPTH, RC, 8, ARCS), F32), vmem((DEPTH, RC, 8, ARCS), F32),
            vmem((N_EX, RC, 8, LN), F32), vmem((N_EX, 2, RC, 8, LN), F32),
            vmem((N_EX, 2, 2, DEPTH, ARCS), F32), vmem((N_EX, 2, 2, DEPTH, ARCS), F32),
            vmem((4, RC, 8, LN), F32), vmem((N_EX, 2, DEPTH, ARCS), F32),
            vmem((2, XC, 8, LN), F32), vmem((2, 2, XC, 8, LN), F32), vmem((2, XC, 8, LN), F32),
            vmem((2, 2, NZ, IY), F32), vmem((2, 2, NZ, IY), F32),
            tiles, msg, vmem((4 * LN, 4 * LN), BF16), vmem((4 * LN, ARCS), BF16),
            vmem((XC, NZ, IY), F32), tiles, tiles, tiles, msg,
            vmem((8, ARCS), F32), tiles, msg, tiles, tiles,
            vmem((XC, NZ, IY), F32),
            sem((15,)), sem((8,)), sem((N_EX + 2, 4)), sem((N_EX + 2, 4)),
            sem((NB,)), sem((NB,)), sem((NH,)), sem((NH,)),
            sem((NB,)), sem((NB,)), sem((NB,)), sem((NB,)), sem((NH,)), sem((NH,)),
        ],
        compiler_params=pltpu.CompilerParams(
            collective_id=0, has_side_effects=True, vmem_limit_bytes=59 * 1024 * 1024
        ),
        name="pylon",
    )(int_temp, int_degree, int_affinity, hum, stemp, sdeg, ambient, colmap.reshape(1, ARCS))
    return pl.pallas_call(
        settle,
        out_shape=outs,
        in_specs=[outside] * 4,
        out_specs=(outside,) * 4,
        scratch_shapes=[vmem(x.shape, F32) for x in outs] + [sem((8,)), sem((8,))],
        compiler_params=pltpu.CompilerParams(vmem_limit_bytes=59 * 1024 * 1024),
        name="settle",
    )(*results)


def solution(mesh):
    plan = P(None, "blk", "ha")
    band = P(None, "ha", "blk")
    return jax.shard_map(
        on_device,
        mesh=mesh,
        in_specs=(plan, plan, plan, band, band, band, P("ha", "blk"), P("blk")),
        out_specs=(plan, plan, band, band),
        check_vma=False,
    )
```

```python
import math

import jax
import jax.numpy as jnp
from jax import lax
from jax.experimental import pallas as pl
from jax.experimental.pallas import tpu as pltpu
from jax.sharding import PartitionSpec as P

F32 = jnp.float32
BF16 = jnp.bfloat16
MESH = pl.DeviceIdType.MESH

NZ, IX, IY = 32, 32, 256
DEPTH, ROWS, ARCS = 16, 64, 256
NB, NH = 32, 4
XC, RC = IX // 8, ROWS // 8
LN = 128

C27 = 2700.0 / 293.15 * math.log2(math.e)
C40 = 4000.0 / 293.15 * math.log2(math.e)

BULK = (0, 1, 2, 3)
WEDGE = (None, 4, 5, 6)
N_EX = 7


def rcp(x):
    r = pl.reciprocal(x, approx=True)
    return r * (2.0 - x * r)


def half_diff(h, t):
    s = 1.0 - h
    s2 = s * s
    s4 = s2 * s2
    q = t * rcp(29.315 + t)
    return (0.00175 + 0.03325 * rcp(1.0 + 65536.0 * (s4 * s4))) * jnp.exp2(C27 * q)


def rates(h, t):
    s = 1.0 - h
    s2 = s * s
    s4 = s2 * s2
    q = t * rcp(29.315 + t)
    d = (0.00175 + 0.03325 * rcp(1.0 + 65536.0 * (s4 * s4))) * jnp.exp2(C27 * q)
    g = 0.08 * rcp(1.0 + 3164.0625 * s4) * jnp.exp2(C40 * q)
    return d, g


def split3(a):
    a1 = a.astype(BF16).astype(F32)
    r1 = a - a1
    a2 = r1.astype(BF16).astype(F32)
    a3 = r1 - a2
    return jnp.concatenate([a1, a2, a3], axis=0).astype(BF16)


def pick(a, b, transpose_b=False):
    rows = a.shape[0]
    dims = (((1,), (1 if transpose_b else 0,)), ((), ()))
    out = lax.dot_general(split3(a), b, dims, preferred_element_type=F32)
    return out[:rows] + out[rows : 2 * rows] + out[2 * rows :]


def both(whole, staged, sems, at, out=False):
    copies = []
    for i in range(2):
        half = slice(i * LN, (i + 1) * LN)
        if len(whole.shape) == 2:
            a, c = whole.at[:, half], staged.at[i]
        else:
            a, c = whole.at[:, :, half], staged.at[:, i]
        src, dst = (c, a) if out else (a, c)
        copies.append(pltpu.make_async_copy(src, dst, sems.at[2 * at + i]))
    return copies


def settle(*refs):
    copies = []
    for i in range(4):
        copies += both(refs[4 + i], refs[i], refs[8], i, True)
    for copy in copies:
        copy.start()
    for copy in copies:
        copy.wait()


def body(
    temp_in, deg_in, aff_in, hum_in, stemp_in, sdeg_in, amb_in, col_in,
    xt, xd, xh, xs,
    xa, xg, xm, col_ref,
    th0, th1, al, hb0, hb1, tb0, tb1, db0, db1, gb, ab,
    cs, cr, rs, rr, cg, dr, ics, icr, icg, irs, irr,
    qs, qr, oh, o2, csum, csend, abuf, ws, rbuf, ub, vs, vr, ss, ubuf, ge,
    in_sem, hs_send, hs_recv, q_send, q_recv, x1_send, x1_recv,
    x2_send, x2_recv, u2_send, u2_recv, u1_send, u1_recv,
):
    b = lax.axis_index("blk")
    ha = lax.axis_index("ha")
    lane = lax.broadcasted_iota(jnp.int32, (8, LN), 1)
    first = lane == 0
    final = lane == LN - 1
    lo, hi = slice(0, LN), slice(LN, 2 * LN)
    zero = jnp.zeros((8, LN), F32)

    halves = (lo, hi)

    col_load = pltpu.make_async_copy(col_in, col_ref, in_sem.at[14])
    col_load.start()
    loads = [
        both(src, dst, in_sem, i)
        for i, (src, dst) in enumerate(
            [
                (temp_in, xt), (hum_in, xh), (stemp_in, xs), (amb_in, xm),
                (aff_in, xa), (deg_in, xd), (sdeg_in, xg),
            ]
        )
    ]
    for copies in loads:
        for copy in copies:
            copy.start()

    barrier = pltpu.get_barrier_semaphore()

    def greet(k, c):
        pl.semaphore_signal(barrier, inc=1, device_id=(lax.rem(b + k, NB), ha), device_id_type=MESH)
        return c

    lax.fori_loop(1, NB, greet, 0)
    for k in range(1, NH):
        pl.semaphore_signal(barrier, inc=1, device_id=(b, lax.rem(ha + k, NH)), device_id_type=MESH)

    def to_blk(src, dst, send, recv):
        def go(k, c):
            to = lax.rem(b + lax.rem(k + 14, NB - 1) + 1, NB)
            pltpu.make_async_remote_copy(
                src_ref=src.at[to // 8], dst_ref=dst.at[b], send_sem=send.at[to],
                recv_sem=recv.at[b], device_id=(to, ha), device_id_type=MESH,
            ).start()
            return c

        lax.fori_loop(1, NB, go, 0)

    def from_blk(src, dst, send, recv):
        def go(k, c):
            other = lax.rem(b + k, NB)
            copy = pltpu.make_async_remote_copy(
                src_ref=src.at[other // 8], dst_ref=dst.at[other], send_sem=send.at[other],
                recv_sem=recv.at[other], device_id=(other, ha), device_id_type=MESH,
            )
            copy.wait_send()
            copy.wait_recv()
            return c

        lax.fori_loop(1, NB, go, 0)
        dst[b] = src[b // 8]

    def combine(buf):
        tiles = []
        for t in range(4):
            acc = zero
            for j in range(8):
                acc = jnp.where((lane >> 4) == ((b + j) & 7), buf[t * 8 + j], acc)
            tiles.append(acc)
        return tiles

    def to_ha(src, dst, send, recv):
        for k in range(1, NH):
            to = lax.rem(ha + k, NH)
            pltpu.make_async_remote_copy(
                src_ref=src.at[to], dst_ref=dst.at[ha], send_sem=send.at[to],
                recv_sem=recv.at[ha], device_id=(b, to), device_id_type=MESH,
            ).start()

    def from_ha(src, dst, send, recv):
        for k in range(1, NH):
            other = lax.rem(ha + k, NH)
            copy = pltpu.make_async_remote_copy(
                src_ref=src.at[other], dst_ref=dst.at[other], send_sem=send.at[other],
                recv_sem=recv.at[other], device_id=(b, other), device_id_type=MESH,
            )
            copy.wait_send()
            copy.wait_recv()
        dst[ha] = src[ha]

    b_dn, b_up = lax.rem(b + NB - 1, NB), lax.rem(b + 1, NB)
    h_dn, h_up = lax.rem(ha + NH - 1, NH), lax.rem(ha + 1, NH)

    def halo(e, src_blk, dst_blk, src_ha, dst_ha):
        return [
            pltpu.make_async_remote_copy(
                src_ref=src, dst_ref=dst, send_sem=hs_send.at[e, i],
                recv_sem=hs_recv.at[e, i], device_id=dev, device_id_type=MESH,
            )
            for i, (src, dst, dev) in enumerate(
                [
                    (src_blk[0], dst_blk.at[1], (b_dn, ha)),
                    (src_blk[1], dst_blk.at[0], (b_up, ha)),
                    (src_ha[0], dst_ha.at[1], (b, h_dn)),
                    (src_ha[1], dst_ha.at[0], (b, h_up)),
                ]
            )
        ]

    def skin_halo(e):
        cols, rows = cs.at[e], rs.at[e]
        return halo(e, (cols, cols), cr.at[e], (rows.at[0], rows.at[1]), rr.at[e])

    def int_halo(e):
        cols, rows = ics.at[e], irs.at[e]
        return halo(N_EX + e, (rows.at[0], rows.at[1]), irr.at[e], (cols, cols), icr.at[e])

    def sweep(go, begin, end, at_once=2):
        count = end - begin

        def some(i, c):
            for j in range(at_once):
                go(begin + at_once * i + j)
            return c

        if count >= at_once:
            lax.fori_loop(0, count // at_once, some, 0)
        for j in range(count % at_once):
            go(end - count % at_once + j)

    def start(copies):
        for copy in copies:
            copy.start()

    def wait(copies):
        for copy in copies:
            copy.wait()

    sub = lax.broadcasted_iota(jnp.int32, (8, LN), 0)

    def put_row(ref, m, row, half):
        tile = pl.ds(pl.multiple_of(((m - 1) // 8) * 8, 8), 8)
        here = sub == lax.rem(m - 1, 8)
        ref[tile, half] = jnp.where(here, jnp.broadcast_to(row, (8, LN)), ref[tile, half])

    pair = (lane + 1) >> 1
    odd = (lane & 1) == 1
    def shift_rows(x, ghost_row, up):
        ghost = jnp.broadcast_to(ghost_row, (8, LN))
        if up:
            return jnp.where(sub == 0, ghost, pltpu.roll(x, 1, 0))
        return jnp.where(sub == 7, ghost, pltpu.roll(x, 7, 0))

    def int_pack(e, m, r, x, mine):
        edge = pltpu.roll(jnp.where(final, x[1], x[0]), 2 * m, 1)
        ics[e, r] = jnp.where(mine, edge, ics[e, r])
        for side, at, k in ((0, 0, 0), (1, XC - 1, 7)):
            if r == at:
                for i, half in enumerate(halves):
                    put_row(irs.at[e, side], m, x[i][k : k + 1], half)

    def int_place(e):
        @pl.when(b == 0)
        def _():
            irr[e, 0] = irs[e, 0]

        @pl.when(b == NB - 1)
        def _():
            irr[e, 1] = irs[e, 1]

        at_low = jnp.full((8, LN), ha, jnp.int32) == 0
        at_high = jnp.full((8, LN), ha, jnp.int32) == NH - 1
        for r in range(XC):
            own = pltpu.roll(ics[e, r], LN - 1, 1)
            low = jnp.where(at_low, own, icr[e, 0, r])
            high = jnp.where(at_high, own, pltpu.roll(icr[e, 1, r], LN - 2, 1))
            icg[e, r] = 0.15 * jnp.where(odd, low, high)

    def sides(x0, x1, ghost):
        a1, b1 = pltpu.roll(x0, 1, 1), pltpu.roll(x1, 1, 1)
        a2, b2 = pltpu.roll(x0, LN - 1, 1), pltpu.roll(x1, LN - 1, 1)
        left = (jnp.where(first, ghost, a1), jnp.where(first, a1, b1))
        right = (jnp.where(final, b2, a2), jnp.where(final, ghost, b2))
        return left, right

    def int_step(src, dst, last):
        for r in range(XC):
            src[0, r] = src[1, r]
            src[NZ + 1, r] = src[NZ, r]

        def go(m):
            for r in range(XC):
                part = pl.ds(r, 8, stride=XC)
                x = [src[m, r, :, half] for half in halves]
                left, right = sides(x[0], x[1], 0.0)
                for i, half in enumerate(halves):
                    t = x[i]
                    if r == 0:
                        up = jnp.where(sub == 0, 0.0, pltpu.roll(src[m, XC - 1, :, half], 1, 0))
                    else:
                        up = src[m, r - 1, :, half]
                    if r == XC - 1:
                        down = jnp.where(sub == 7, 0.0, pltpu.roll(src[m, 0, :, half], 7, 0))
                    else:
                        down = src[m, r + 1, :, half]
                    total = (left[i] + right[i]) + (up + down) + (
                        src[m - 1, r, :, half] + src[m + 1, r, :, half]
                    )
                    alpha = al[m - 1, r, :, half] if last else xd[m - 1, i, part, :]
                    rate = jnp.exp2(C40 * (t * rcp(29.315 + t)))
                    rise = xa[m - 1, i, part, :] * (0.85 - alpha) * rate
                    if last:
                        xd[m - 1, i, part, :] = alpha + rise
                    else:
                        al[m - 1, r, :, half] = alpha + rise
                    dst[m, r, :, half] = t + 0.15 * (total - 6.0 * t) + 4.0 * rise

        sweep(go, 1, NZ + 1, 4)

    def int_fix(e, dst, last):
        def go(m):
            mine = pair == m
            sums = [0.0, 0.0]
            for r in range(XC):
                ghost = pltpu.roll(icg[e, r], 129 - 2 * m, 1)
                new = []
                for i, half in enumerate(halves):
                    out = dst[m, r, :, half] + jnp.where(final if i else first, ghost, 0.0)
                    for side, at, k in ((0, 0, 0), (1, XC - 1, 7)):
                        if r == at:
                            row = jnp.broadcast_to(irr[e, side, pl.ds(m - 1, 1), :][:, half], (8, LN))
                            out = out + jnp.where(sub == k, 0.15 * row, 0.0)
                    dst[m, r, :, half] = out
                    sums[i] = sums[i] + out
                    new.append(out)
                if not last:
                    int_pack(1, m, r, new, mine)
            if last:
                for i, half in enumerate(halves):
                    pairs = sums[i] + pltpu.roll(sums[i], 7, 0)
                    for r in range(XC):
                        put_row(csum.at[r], m, pairs[2 * r : 2 * r + 1], half)

        sweep(go, 1, NZ + 1, 4)

    states = ((hb0, tb0, db0), (hb1, tb1, db1))

    def skin_pack(e, m, r, h, t, mine_h, mine_t):
        eh = pltpu.roll(jnp.where(final, h[1], h[0]), 2 * m, 1)
        et = pltpu.roll(jnp.where(final, t[1], t[0]), 2 * m + 40, 1)
        cs[e, r] = jnp.where(mine_t, et, jnp.where(mine_h, eh, cs[e, r]))
        for side, at, k in ((0, 0, 0), (1, RC - 1, 7)):
            if r == at:
                for f, x in enumerate((h, t)):
                    for i, half in enumerate(halves):
                        put_row(rs.at[e, side, f], m, x[i][k : k + 1], half)

    def skin_air(buf):
        H, T, D = buf
        for r in range(RC):
            t = T[DEPTH, r]
            T[DEPTH + 1, r] = t
            D[DEPTH + 1, r] = half_diff(H[DEPTH + 1, r], t)

    def skin_first():
        H, T, D = states[0]
        for r in range(RC):
            for i, half in enumerate(halves):
                air = xm[i, pl.ds(r, 8, stride=RC), :]
                for buf in (hb0, hb1):
                    buf[0, r, :, half] = jnp.ones((8, LN), F32)
                    buf[DEPTH + 1, r, :, half] = air

        def go(m, c):
            mine_h, mine_t = pair == m, pair == m + 20
            for r in range(RC):
                part = pl.ds(r, 8, stride=RC)
                h = [xh[m - 1, i, part, :] for i in range(2)]
                t = [xs[m - 1, i, part, :] for i in range(2)]
                for i, half in enumerate(halves):
                    d, g = rates(h[i], t[i])
                    H[m, r, :, half] = h[i]
                    T[m, r, :, half] = t[i]
                    D[m, r, :, half] = d
                    gb[m - 1, r, :, half] = g
                skin_pack(0, m, r, h, t, mine_h, mine_t)
            return c

        lax.fori_loop(1, DEPTH + 1, go, 0)
        skin_air(states[0])

    def skin_place(k, e, wedge):
        @pl.when(ha == 0)
        def _():
            rr[e, 0] = rs[e, 0]

        @pl.when(ha == NH - 1)
        def _():
            rr[e, 1] = rs[e, 1]

        if wedge:
            here = lax.broadcasted_iota(jnp.int32, (DEPTH, ARCS), 0) >= k
            for side in range(2):
                for f in range(2):
                    rr[e, side, f] = jnp.where(here, rr[BULK[k], side, f], rr[e, side, f])
        for side in range(2):
            dr[e, side] = half_diff(rr[e, side, 0], rr[e, side, 1])
        field = jnp.where(lane >= 80, lane - 80, jnp.where(lane >= 40, lane - 40, lane))
        fresh = (field >> 1) < k
        for r in range(RC):
            x = jnp.where(odd, cr[e, 0, r], pltpu.roll(cr[e, 1, r], LN - 2, 1))
            d = half_diff(x, pltpu.roll(x, LN - 40, 1))
            x = jnp.where(lane >= 80, pltpu.roll(d, 80, 1), x)
            cg[k, r] = jnp.where(fresh, x, cg[k, r]) if wedge else x

    def skin_step(k, begin, end, e, e_in):
        H, T, D = states[k % 2]
        Hn, Tn, Dn = states[(k + 1) % 2]

        def go(m):
            mine_h, mine_t = pair == m, pair == m + 20
            air = jnp.where(m == DEPTH, 2.0, 0.0)
            row = pl.ds(m - 1, 1)
            flow = [0.0, 0.0]
            for r in range(RC):
                part = pl.ds(r, 8, stride=RC)
                ghosts = cg[k, r]
                h = [H[m, r, :, half] for half in halves]
                t = [T[m, r, :, half] for half in halves]
                d = [D[m, r, :, half] for half in halves]
                gh, gt, gd = (pltpu.roll(ghosts, at - 2 * m, 1) for at in (129, 89, 49))
                tl, tr = sides(t[0], t[1], gt)
                h0, h1 = pltpu.roll(h[0], LN - 1, 1), pltpu.roll(h[1], LN - 1, 1)
                d0, d1 = pltpu.roll(d[0], LN - 1, 1), pltpu.roll(d[1], LN - 1, 1)
                f0 = (d[0] + jnp.where(final, d1, d0)) * (jnp.where(final, h1, h0) - h[0])
                f1 = (d[1] + jnp.where(final, gd, d1)) * (jnp.where(final, gh, h1) - h[1])
                s0, s1 = pltpu.roll(f0, 1, 1), pltpu.roll(f1, 1, 1)
                across = (
                    f0 - jnp.where(first, (d[0] + gd) * (h[0] - gh), s0),
                    f1 - jnp.where(first, s0, s1),
                )
                hn, tn = [], []
                for i, half in enumerate(halves):
                    hc, tc, dc = h[i], t[i], d[i]
                    if r == 0:
                        hu, tu, du = (
                            shift_rows(x[m, RC - 1, :, half], g[row, :][:, half], True)
                            for x, g in ((H, rr.at[e_in, 0, 0]), (T, rr.at[e_in, 0, 1]), (D, dr.at[e_in, 0]))
                        )
                        flow[i] = (du + dc) * (hc - hu)
                    else:
                        tu = T[m, r - 1, :, half]
                    if r == RC - 1:
                        hd, td, dd = (
                            shift_rows(x[m, 0, :, half], g[row, :][:, half], False)
                            for x, g in ((H, rr.at[e_in, 1, 0]), (T, rr.at[e_in, 1, 1]), (D, dr.at[e_in, 1]))
                        )
                    else:
                        hd, td, dd = H[m, r + 1, :, half], T[m, r + 1, :, half], D[m, r + 1, :, half]
                    below = (dc + dd) * (hd - hc)
                    out = (dc + D[m + 1, r, :, half]) * (H[m + 1, r, :, half] - hc)
                    into = (dc + D[m - 1, r, :, half]) * (H[m - 1, r, :, half] - hc)
                    moist = (out + into) + (below - flow[i]) + across[i]
                    flow[i] = below
                    total = (T[m + 1, r, :, half] + T[m - 1, r, :, half]) + (tu + td) + (tl[i] + tr[i])
                    a = xg[m - 1, i, part, :] if k == 0 else ab[m - 1, r, :, half]
                    hyd = gb[m - 1, r, :, half] * (0.85 - a)
                    h1_ = hc + moist - 0.3 * hyd
                    t1_ = tc + 0.15 * (total - 6.0 * tc) + 4.0 * hyd + air * out
                    if k < 3:
                        Hn[m, r, :, half] = h1_
                        Tn[m, r, :, half] = t1_
                        ab[m - 1, r, :, half] = a + hyd
                        dn, gn = rates(h1_, t1_)
                        Dn[m, r, :, half] = dn
                        gb[m - 1, r, :, half] = gn
                    else:
                        xh[m - 1, i, part, :] = h1_
                        xs[m - 1, i, part, :] = t1_
                    hn.append(h1_)
                    tn.append(t1_)
                if k < 3:
                    skin_pack(e, m, r, hn, tn, mine_h, mine_t)

        sweep(go, begin + 1, end + 1)
        if end == DEPTH and k < 3:
            skin_air(states[(k + 1) % 2])

    def inflow(k):
        T = states[k % 2][1]
        gain = 0.0 if k == 0 else ub[...]
        for r in range(RC):
            gain = gain + (T[0, r] - T[1, r])
        ub[...] = gain

    for e in range(2):
        for r in range(XC):
            ics[e, r] = zero
    wait(loads[0])

    def pack0(m, c):
        mine = pair == m
        for r in range(XC):
            x = [xt[m - 1, i, pl.ds(r, 8, stride=XC), :] for i in range(2)]
            for i, half in enumerate(halves):
                th0[m, r, :, half] = x[i]
            int_pack(0, m, r, x, mine)
        return c

    lax.fori_loop(1, NZ + 1, pack0, 0, unroll=2)
    pl.semaphore_wait(barrier, NB - 1 + NH - 1)
    ex_i0 = int_halo(0)
    start(ex_i0)

    col_load.wait()

    col = col_ref[...]
    owner = col >> 7
    colf = jnp.broadcast_to(owner.astype(F32), (ARCS, ARCS))
    owner_down = colf.T
    q_i = lax.broadcasted_iota(jnp.int32, (ARCS, ARCS), 0)
    p_i = lax.broadcasted_iota(jnp.int32, (ARCS, ARCS), 1)
    earlier = jnp.where((owner_down == colf) & (q_i < p_i), 1.0, 0.0)
    rank = jnp.sum(earlier, axis=0, keepdims=True).astype(jnp.int32)
    ob = col >> 9
    pos = (ob >> 3) * LN + (((ob + b) & 7) << 4) + ((owner & 3) << 2) + rank
    posf = pos.astype(F32)
    pos_down = jnp.broadcast_to(posf, (LN, ARCS)).T
    val_down = jnp.broadcast_to((col & 511).astype(F32) + 1.0, (LN, ARCS)).T
    lanes_a = lax.broadcasted_iota(jnp.int32, (ARCS, LN), 1).astype(F32)
    for t in range(4):
        hit = jnp.where(pos_down == lanes_a + float(t * LN), val_down, 0.0)
        qs[t] = jnp.broadcast_to(jnp.sum(hit, axis=0, keepdims=True) - 1.0, (8, LN))
    slot_i = lax.broadcasted_iota(jnp.int32, (4 * LN, ARCS), 0).astype(F32)
    o2[...] = jnp.where(slot_i == posf, 1.0, 0.0).astype(BF16)

    def clear(e, c):
        for side in range(2):
            for r in range(RC):
                cs[e, r] = zero
            for f in range(2):
                rs[e, side, f] = jnp.zeros((DEPTH, ARCS), F32)
        return c

    lax.fori_loop(0, N_EX, clear, 0)
    to_blk(qs, qr, q_send, q_recv)
    for i in (1, 2, 3):
        wait(loads[i])
    skin_first()
    ex_s0 = skin_halo(0)
    start(ex_s0)

    wait(loads[4])
    wait(loads[5])
    int_step(th0, th1, False)
    wait(ex_i0)
    int_place(0)
    int_fix(0, th1, False)
    ex_i1 = int_halo(1)
    start(ex_i1)
    int_step(th1, th0, True)

    wait(loads[6])
    wait(ex_s0)
    skin_place(0, 0, False)
    skin_step(0, 1, DEPTH, BULK[1], BULK[0])
    ex_b1 = skin_halo(BULK[1])
    start(ex_b1)

    wait(ex_i1)
    int_place(1)
    int_fix(1, th0, True)
    y_i = lax.broadcasted_iota(jnp.int32, (IY, LN), 0)
    c_i = lax.broadcasted_iota(jnp.int32, (IY, LN), 1)

    def mean_matrix(i):
        return jnp.where(((c_i >> 5) == i) & ((c_i & 31) == (y_i >> 3)), 1.0 / 64.0, 0.0).astype(BF16)

    coarse = jnp.zeros((NZ, LN), F32)
    for i in range(XC):
        coarse = coarse + pick(csum[i], mean_matrix(i))
    for i in range(NH):
        csend[i] = coarse[8 * i : 8 * i + 8]
    to_ha(csend, abuf, x1_send, x1_recv)

    from_blk(qs, qr, q_send, q_recv)
    slots = combine(qr)
    for t in range(4):
        key = jnp.broadcast_to(slots[t][0:1], (4 * LN, LN))
        row = lax.broadcasted_iota(jnp.int32, (4 * LN, LN), 0).astype(F32)
        oh[:, t * LN : (t + 1) * LN] = jnp.where(row == key, 1.0, 0.0).astype(BF16)

    wait(ex_b1)
    skin_place(1, BULK[1], False)

    from_ha(csend, abuf, x1_send, x1_recv)
    wide = pick(jnp.concatenate([abuf[i] for i in range(NH)], axis=1), oh[...])
    for t in range(4):
        ws[t] = wide[:, t * LN : (t + 1) * LN]
    to_blk(ws, rbuf, x2_send, x2_recv)

    skin_step(1, 2, DEPTH, BULK[2], BULK[1])
    ex_b2 = skin_halo(BULK[2])
    start(ex_b2)

    from_blk(ws, rbuf, x2_send, x2_recv)
    bound = pick(jnp.concatenate(combine(rbuf), axis=1), o2[...])
    bound_d = half_diff(jnp.ones((8, ARCS), F32), bound)
    for r in range(RC):
        for _, T, D in states:
            T[0, r] = bound
            D[0, r] = bound_d

    inflow(0)
    skin_step(0, 0, 1, WEDGE[1], BULK[0])
    ex_w1 = skin_halo(WEDGE[1])
    start(ex_w1)
    inflow(1)

    wait(ex_b2)
    skin_place(2, BULK[2], False)
    skin_step(2, 3, DEPTH, BULK[3], BULK[2])
    ex_b3 = skin_halo(BULK[3])
    start(ex_b3)

    wait(ex_w1)
    skin_place(1, WEDGE[1], True)
    skin_step(1, 0, 2, WEDGE[2], WEDGE[1])
    ex_w2 = skin_halo(WEDGE[2])
    start(ex_w2)
    inflow(2)

    wait(ex_b3)
    skin_place(3, BULK[3], False)
    skin_step(3, 10, DEPTH, None, BULK[3])

    wait(ex_w2)
    skin_place(2, WEDGE[2], True)
    skin_step(2, 0, 3, WEDGE[3], WEDGE[2])
    ex_w3 = skin_halo(WEDGE[3])
    start(ex_w3)
    inflow(3)
    heat = pick(0.15 * ub[...], o2[...], transpose_b=True)
    for t in range(4):
        vs[t] = heat[:, t * LN : (t + 1) * LN]
    to_blk(vs, vr, u2_send, u2_recv)

    skin_step(3, 4, 10, None, BULK[3])
    wait(ex_w3)
    skin_place(3, WEDGE[3], True)

    from_blk(vs, vr, u2_send, u2_recv)
    summed = pick(jnp.concatenate(combine(vr), axis=1), oh[...], transpose_b=True)
    for i in range(NH):
        ss[i] = summed[:, i * LN : (i + 1) * LN]
    to_ha(ss, ubuf, u1_send, u1_recv)

    skin_step(3, 0, 4, None, WEDGE[3])

    from_ha(ss, ubuf, u1_send, u1_recv)
    uptake = jnp.concatenate([ubuf[i] for i in range(NH)], axis=0)
    for i in range(XC):
        ge[i] = 0.5 * pick(uptake, mean_matrix(i), transpose_b=True)

    def finish(m, c):
        for i, half in enumerate(halves):
            cool = jnp.zeros((8, LN), F32)
            for g in range(XC):
                row = jnp.broadcast_to(ge[g, pl.ds(m - 1, 1), :][:, half], (8, LN))
                cool = jnp.where((sub >> 1) == g, row, cool)
            for r in range(XC):
                xt[m - 1, i, pl.ds(r, 8, stride=XC), :] = th0[m, r, :, half] - cool
        return c

    lax.fori_loop(1, NZ + 1, finish, 0, unroll=2)


def on_device(int_temp, int_degree, int_affinity, hum, stemp, sdeg, ambient, colmap):
    vmem = pltpu.VMEM
    sem = pltpu.SemaphoreType.DMA
    skin_buf = vmem((DEPTH + 2, RC, 8, ARCS), F32)
    int_buf = vmem((NZ + 2, XC, 8, IY), F32)
    int_stage = vmem((NZ, 2, IX, LN), F32)
    skin_stage = vmem((DEPTH, 2, ROWS, LN), F32)
    outside = pl.BlockSpec(memory_space=pltpu.HBM)
    interior = jax.ShapeDtypeStruct((NZ, IX, IY), F32)
    skin = jax.ShapeDtypeStruct((DEPTH, ROWS, ARCS), F32)
    outs = (interior, interior, skin, skin)
    msg = vmem((NB, 8, LN), F32)
    tiles = vmem((4, 8, LN), F32)
    inside = pl.BlockSpec(memory_space=pltpu.VMEM)
    int_half = jax.ShapeDtypeStruct((NZ, 2, IX, LN), F32)
    skin_half = jax.ShapeDtypeStruct((DEPTH, 2, ROWS, LN), F32)
    results = pl.pallas_call(
        body,
        out_shape=(int_half, int_half, skin_half, skin_half),
        in_specs=[outside] * 8,
        out_specs=(inside,) * 4,
        scratch_shapes=[
            int_stage, skin_stage,
            vmem((2, ROWS, LN), F32), vmem((1, ARCS), jnp.int32),
            int_buf, int_buf, vmem((NZ, XC, 8, IY), F32),
            skin_buf, skin_buf, skin_buf, skin_buf, skin_buf, skin_buf,
            vmem((DEPTH, RC, 8, ARCS), F32), vmem((DEPTH, RC, 8, ARCS), F32),
            vmem((N_EX, RC, 8, LN), F32), vmem((N_EX, 2, RC, 8, LN), F32),
            vmem((N_EX, 2, 2, DEPTH, ARCS), F32), vmem((N_EX, 2, 2, DEPTH, ARCS), F32),
            vmem((4, RC, 8, LN), F32), vmem((N_EX, 2, DEPTH, ARCS), F32),
            vmem((2, XC, 8, LN), F32), vmem((2, 2, XC, 8, LN), F32), vmem((2, XC, 8, LN), F32),
            vmem((2, 2, NZ, IY), F32), vmem((2, 2, NZ, IY), F32),
            tiles, msg, vmem((4 * LN, 4 * LN), BF16), vmem((4 * LN, ARCS), BF16),
            vmem((XC, NZ, IY), F32), tiles, tiles, tiles, msg,
            vmem((8, ARCS), F32), tiles, msg, tiles, tiles,
            vmem((XC, NZ, IY), F32),
            sem((15,)), sem((N_EX + 2, 4)), sem((N_EX + 2, 4)),
            sem((NB,)), sem((NB,)), sem((NH,)), sem((NH,)),
            sem((NB,)), sem((NB,)), sem((NB,)), sem((NB,)), sem((NH,)), sem((NH,)),
        ],
        compiler_params=pltpu.CompilerParams(
            collective_id=0, has_side_effects=True, vmem_limit_bytes=50944 * 1024
        ),
        name="pylon",
    )(*(
        pltpu.with_memory_space_constraint(x, pltpu.HBM)
        for x in (int_temp, int_degree, int_affinity, hum, stemp, sdeg, ambient, colmap.reshape(1, ARCS))
    ))
    return pl.pallas_call(
        settle,
        out_shape=outs,
        in_specs=[inside] * 4,
        out_specs=(outside,) * 4,
        scratch_shapes=[sem((8,))],
        compiler_params=pltpu.CompilerParams(vmem_limit_bytes=8 * 1024 * 1024),
        name="settle",
    )(*results)


def solution(mesh):
    plan = P(None, "blk", "ha")
    band = P(None, "ha", "blk")
    return jax.shard_map(
        on_device,
        mesh=mesh,
        in_specs=(plan, plan, plan, band, band, band, P("ha", "blk"), P("blk")),
        out_specs=(plan, plan, band, band),
        check_vma=False,
    )
```

```python
import math

import jax
import jax.numpy as jnp
from jax import lax
from jax.experimental import pallas as pl
from jax.experimental.pallas import tpu as pltpu
from jax.sharding import PartitionSpec as P

F32 = jnp.float32
BF16 = jnp.bfloat16
MESH = pl.DeviceIdType.MESH

NZ, IX, IY = 32, 32, 256
DEPTH, ROWS, ARCS = 16, 64, 256
NB, NH = 32, 4
XC, RC = IX // 8, ROWS // 8
LN = 128

C27 = 2700.0 / 293.15 * math.log2(math.e)
C40 = 4000.0 / 293.15 * math.log2(math.e)

BULK = (0, 1, 2, 3)
WEDGE = (None, 4, 5, 6)
N_EX = 7


def rcp(x):
    r = pl.reciprocal(x, approx=True)
    return r * (2.0 - x * r)


def half_diff(h, t):
    s = 1.0 - h
    s2 = s * s
    s4 = s2 * s2
    q = t * rcp(29.315 + t)
    return (0.00175 + 0.03325 * rcp(1.0 + 65536.0 * (s4 * s4))) * jnp.exp2(C27 * q)


def rates(h, t):
    s = 1.0 - h
    s2 = s * s
    s4 = s2 * s2
    q = t * rcp(29.315 + t)
    d = (0.00175 + 0.03325 * rcp(1.0 + 65536.0 * (s4 * s4))) * jnp.exp2(C27 * q)
    g = 0.08 * rcp(1.0 + 3164.0625 * s4) * jnp.exp2(C40 * q)
    return d, g


def split3(a):
    a1 = a.astype(BF16).astype(F32)
    r1 = a - a1
    a2 = r1.astype(BF16).astype(F32)
    a3 = r1 - a2
    return jnp.concatenate([a1, a2, a3], axis=0).astype(BF16)


def pick(a, b, transpose_b=False):
    rows = a.shape[0]
    dims = (((1,), (1 if transpose_b else 0,)), ((), ()))
    out = lax.dot_general(split3(a), b, dims, preferred_element_type=F32)
    return out[:rows] + out[rows : 2 * rows] + out[2 * rows :]


def both(whole, staged, sems, at, out=False):
    copies = []
    for i in range(2):
        half = slice(i * LN, (i + 1) * LN)
        if len(whole.shape) == 2:
            a, c = whole.at[:, half], staged.at[i]
        else:
            a, c = whole.at[:, :, half], staged.at[:, i]
        src, dst = (c, a) if out else (a, c)
        copies.append(pltpu.make_async_copy(src, dst, sems.at[2 * at + i]))
    return copies


def settle(*refs):
    copies = []
    for i in range(4):
        copies += both(refs[4 + i], refs[i], refs[8], i, True)
    for copy in copies:
        copy.start()
    for copy in copies:
        copy.wait()


def body(
    temp_in, deg_in, aff_in, hum_in, stemp_in, sdeg_in, amb_in, col_in,
    xt, xd, xh, xs,
    xa, xg, xm, col_ref,
    th0, th1, al, hb0, hb1, tb0, tb1, db0, db1, gb, ab,
    cs, cr, rs, rr, cg, dr, ics, icr, icg, irs, irr,
    qs, qr, oh, o2, csum, csend, abuf, ws, rbuf, ub, vs, vr, ss, ubuf, ge,
    in_sem, hs_send, hs_recv, q_send, q_recv, x1_send, x1_recv,
    x2_send, x2_recv, u2_send, u2_recv, u1_send, u1_recv,
):
    b = lax.axis_index("blk")
    ha = lax.axis_index("ha")
    lane = lax.broadcasted_iota(jnp.int32, (8, LN), 1)
    first = lane == 0
    final = lane == LN - 1
    lo, hi = slice(0, LN), slice(LN, 2 * LN)
    zero = jnp.zeros((8, LN), F32)

    halves = (lo, hi)

    col_load = pltpu.make_async_copy(col_in, col_ref, in_sem.at[14])
    col_load.start()
    loads = [
        both(src, dst, in_sem, i)
        for i, (src, dst) in enumerate(
            [
                (temp_in, xt), (hum_in, xh), (stemp_in, xs), (amb_in, xm),
                (aff_in, xa), (deg_in, xd), (sdeg_in, xg),
            ]
        )
    ]
    for copies in loads:
        for copy in copies:
            copy.start()

    barrier = pltpu.get_barrier_semaphore()

    def greet(k, c):
        pl.semaphore_signal(barrier, inc=1, device_id=(lax.rem(b + k, NB), ha), device_id_type=MESH)
        return c

    lax.fori_loop(1, NB, greet, 0)
    for k in range(1, NH):
        pl.semaphore_signal(barrier, inc=1, device_id=(b, lax.rem(ha + k, NH)), device_id_type=MESH)

    def to_blk(src, dst, send, recv):
        def go(k, c):
            to = lax.rem(b + lax.rem(k + 14, NB - 1) + 1, NB)
            pltpu.make_async_remote_copy(
                src_ref=src.at[to // 8], dst_ref=dst.at[b], send_sem=send.at[to],
                recv_sem=recv.at[b], device_id=(to, ha), device_id_type=MESH,
            ).start()
            return c

        lax.fori_loop(1, NB, go, 0)

    def from_blk(src, dst, send, recv):
        def go(k, c):
            other = lax.rem(b + k, NB)
            copy = pltpu.make_async_remote_copy(
                src_ref=src.at[other // 8], dst_ref=dst.at[other], send_sem=send.at[other],
                recv_sem=recv.at[other], device_id=(other, ha), device_id_type=MESH,
            )
            copy.wait_send()
            copy.wait_recv()
            return c

        lax.fori_loop(1, NB, go, 0)
        dst[b] = src[b // 8]

    def combine(buf):
        tiles = []
        for t in range(4):
            acc = zero
            for j in range(8):
                acc = jnp.where((lane >> 4) == ((b + j) & 7), buf[t * 8 + j], acc)
            tiles.append(acc)
        return tiles

    def to_ha(src, dst, send, recv):
        for k in range(1, NH):
            to = lax.rem(ha + k, NH)
            pltpu.make_async_remote_copy(
                src_ref=src.at[to], dst_ref=dst.at[ha], send_sem=send.at[to],
                recv_sem=recv.at[ha], device_id=(b, to), device_id_type=MESH,
            ).start()

    def from_ha(src, dst, send, recv):
        for k in range(1, NH):
            other = lax.rem(ha + k, NH)
            copy = pltpu.make_async_remote_copy(
                src_ref=src.at[other], dst_ref=dst.at[other], send_sem=send.at[other],
                recv_sem=recv.at[other], device_id=(b, other), device_id_type=MESH,
            )
            copy.wait_send()
            copy.wait_recv()
        dst[ha] = src[ha]

    b_dn, b_up = lax.rem(b + NB - 1, NB), lax.rem(b + 1, NB)
    h_dn, h_up = lax.rem(ha + NH - 1, NH), lax.rem(ha + 1, NH)

    def halo(e, src_blk, dst_blk, src_ha, dst_ha):
        return [
            pltpu.make_async_remote_copy(
                src_ref=src, dst_ref=dst, send_sem=hs_send.at[e, i],
                recv_sem=hs_recv.at[e, i], device_id=dev, device_id_type=MESH,
            )
            for i, (src, dst, dev) in enumerate(
                [
                    (src_blk[0], dst_blk.at[1], (b_dn, ha)),
                    (src_blk[1], dst_blk.at[0], (b_up, ha)),
                    (src_ha[0], dst_ha.at[1], (b, h_dn)),
                    (src_ha[1], dst_ha.at[0], (b, h_up)),
                ]
            )
        ]

    def skin_halo(e):
        cols, rows = cs.at[e], rs.at[e]
        return halo(e, (cols, cols), cr.at[e], (rows.at[0], rows.at[1]), rr.at[e])

    def int_halo(e):
        cols, rows = ics.at[e], irs.at[e]
        return halo(N_EX + e, (rows.at[0], rows.at[1]), irr.at[e], (cols, cols), icr.at[e])

    def sweep(go, begin, end, at_once=2):
        count = end - begin

        def some(i, c):
            for j in range(at_once):
                go(begin + at_once * i + j)
            return c

        if count >= at_once:
            lax.fori_loop(0, count // at_once, some, 0)
        for j in range(count % at_once):
            go(end - count % at_once + j)

    def start(copies):
        for copy in copies:
            copy.start()

    def wait(copies):
        for copy in copies:
            copy.wait()

    sub = lax.broadcasted_iota(jnp.int32, (8, LN), 0)

    def put_row(ref, m, row, half):
        tile = pl.ds(pl.multiple_of(((m - 1) // 8) * 8, 8), 8)
        here = sub == lax.rem(m - 1, 8)
        ref[tile, half] = jnp.where(here, jnp.broadcast_to(row, (8, LN)), ref[tile, half])

    pair = (lane + 1) >> 1
    odd = (lane & 1) == 1
    def shift_rows(x, ghost_row, up):
        ghost = jnp.broadcast_to(ghost_row, (8, LN))
        if up:
            return jnp.where(sub == 0, ghost, pltpu.roll(x, 1, 0))
        return jnp.where(sub == 7, ghost, pltpu.roll(x, 7, 0))

    def int_pack(e, m, r, x, mine):
        edge = pltpu.roll(jnp.where(final, x[1], x[0]), 2 * m, 1)
        ics[e, r] = jnp.where(mine, edge, ics[e, r])
        for side, at, k in ((0, 0, 0), (1, XC - 1, 7)):
            if r == at:
                for i, half in enumerate(halves):
                    put_row(irs.at[e, side], m, x[i][k : k + 1], half)

    def int_place(e):
        @pl.when(b == 0)
        def _():
            irr[e, 0] = irs[e, 0]

        @pl.when(b == NB - 1)
        def _():
            irr[e, 1] = irs[e, 1]

        at_low = jnp.full((8, LN), ha, jnp.int32) == 0
        at_high = jnp.full((8, LN), ha, jnp.int32) == NH - 1
        for r in range(XC):
            own = pltpu.roll(ics[e, r], LN - 1, 1)
            low = jnp.where(at_low, own, icr[e, 0, r])
            high = jnp.where(at_high, own, pltpu.roll(icr[e, 1, r], LN - 2, 1))
            icg[e, r] = 0.15 * jnp.where(odd, low, high)

    def sides(x0, x1, ghost):
        a1, b1 = pltpu.roll(x0, 1, 1), pltpu.roll(x1, 1, 1)
        a2, b2 = pltpu.roll(x0, LN - 1, 1), pltpu.roll(x1, LN - 1, 1)
        left = (jnp.where(first, ghost, a1), jnp.where(first, a1, b1))
        right = (jnp.where(final, b2, a2), jnp.where(final, ghost, b2))
        return left, right

    def int_step(src, dst, last):
        for r in range(XC):
            src[0, r] = src[1, r]
            src[NZ + 1, r] = src[NZ, r]

        def go(m):
            for r in range(XC):
                part = pl.ds(r, 8, stride=XC)
                x = [src[m, r, :, half] for half in halves]
                left, right = sides(x[0], x[1], 0.0)
                for i, half in enumerate(halves):
                    t = x[i]
                    if r == 0:
                        up = jnp.where(sub == 0, 0.0, pltpu.roll(src[m, XC - 1, :, half], 1, 0))
                    else:
                        up = src[m, r - 1, :, half]
                    if r == XC - 1:
                        down = jnp.where(sub == 7, 0.0, pltpu.roll(src[m, 0, :, half], 7, 0))
                    else:
                        down = src[m, r + 1, :, half]
                    total = (left[i] + right[i]) + (up + down) + (
                        src[m - 1, r, :, half] + src[m + 1, r, :, half]
                    )
                    alpha = al[m - 1, r, :, half] if last else xd[m - 1, i, part, :]
                    rate = jnp.exp2(C40 * (t * rcp(29.315 + t)))
                    rise = xa[m - 1, i, part, :] * (0.85 - alpha) * rate
                    if last:
                        xd[m - 1, i, part, :] = alpha + rise
                    else:
                        al[m - 1, r, :, half] = alpha + rise
                    dst[m, r, :, half] = t + 0.15 * (total - 6.0 * t) + 4.0 * rise

        sweep(go, 1, NZ + 1, 4)

    def int_fix(e, dst, last):
        def go(m):
            mine = pair == m
            sums = [0.0, 0.0]
            for r in range(XC):
                ghost = pltpu.roll(icg[e, r], 129 - 2 * m, 1)
                new = []
                for i, half in enumerate(halves):
                    out = dst[m, r, :, half] + jnp.where(final if i else first, ghost, 0.0)
                    for side, at, k in ((0, 0, 0), (1, XC - 1, 7)):
                        if r == at:
                            row = jnp.broadcast_to(irr[e, side, pl.ds(m - 1, 1), :][:, half], (8, LN))
                            out = out + jnp.where(sub == k, 0.15 * row, 0.0)
                    dst[m, r, :, half] = out
                    sums[i] = sums[i] + out
                    new.append(out)
                if not last:
                    int_pack(1, m, r, new, mine)
            if last:
                for i, half in enumerate(halves):
                    pairs = sums[i] + pltpu.roll(sums[i], 7, 0)
                    for r in range(XC):
                        put_row(csum.at[r], m, pairs[2 * r : 2 * r + 1], half)

        sweep(go, 1, NZ + 1, 4)

    states = ((hb0, tb0, db0), (hb1, tb1, db1))

    def skin_pack(e, m, r, h, t, mine_h, mine_t):
        eh = pltpu.roll(jnp.where(final, h[1], h[0]), 2 * m, 1)
        et = pltpu.roll(jnp.where(final, t[1], t[0]), 2 * m + 40, 1)
        cs[e, r] = jnp.where(mine_t, et, jnp.where(mine_h, eh, cs[e, r]))
        for side, at, k in ((0, 0, 0), (1, RC - 1, 7)):
            if r == at:
                for f, x in enumerate((h, t)):
                    for i, half in enumerate(halves):
                        put_row(rs.at[e, side, f], m, x[i][k : k + 1], half)

    def skin_air(buf):
        H, T, D = buf
        for r in range(RC):
            t = T[DEPTH, r]
            T[DEPTH + 1, r] = t
            D[DEPTH + 1, r] = half_diff(H[DEPTH + 1, r], t)

    def skin_first():
        H, T, D = states[0]
        for r in range(RC):
            for i, half in enumerate(halves):
                air = xm[i, pl.ds(r, 8, stride=RC), :]
                for buf in (hb0, hb1):
                    buf[0, r, :, half] = jnp.ones((8, LN), F32)
                    buf[DEPTH + 1, r, :, half] = air

        def go(m, c):
            mine_h, mine_t = pair == m, pair == m + 20
            for r in range(RC):
                part = pl.ds(r, 8, stride=RC)
                h = [xh[m - 1, i, part, :] for i in range(2)]
                t = [xs[m - 1, i, part, :] for i in range(2)]
                for i, half in enumerate(halves):
                    d, g = rates(h[i], t[i])
                    H[m, r, :, half] = h[i]
                    T[m, r, :, half] = t[i]
                    D[m, r, :, half] = d
                    gb[m - 1, r, :, half] = g
                skin_pack(0, m, r, h, t, mine_h, mine_t)
            return c

        lax.fori_loop(1, DEPTH + 1, go, 0)
        skin_air(states[0])

    def skin_place(k, e, wedge):
        @pl.when(ha == 0)
        def _():
            rr[e, 0] = rs[e, 0]

        @pl.when(ha == NH - 1)
        def _():
            rr[e, 1] = rs[e, 1]

        if wedge:
            here = lax.broadcasted_iota(jnp.int32, (DEPTH, ARCS), 0) >= k
            for side in range(2):
                for f in range(2):
                    rr[e, side, f] = jnp.where(here, rr[BULK[k], side, f], rr[e, side, f])
        for side in range(2):
            dr[e, side] = half_diff(rr[e, side, 0], rr[e, side, 1])
        field = jnp.where(lane >= 80, lane - 80, jnp.where(lane >= 40, lane - 40, lane))
        fresh = (field >> 1) < k
        for r in range(RC):
            x = jnp.where(odd, cr[e, 0, r], pltpu.roll(cr[e, 1, r], LN - 2, 1))
            d = half_diff(x, pltpu.roll(x, LN - 40, 1))
            x = jnp.where(lane >= 80, pltpu.roll(d, 80, 1), x)
            cg[k, r] = jnp.where(fresh, x, cg[k, r]) if wedge else x

    def skin_step(k, begin, end, e, e_in):
        H, T, D = states[k % 2]
        Hn, Tn, Dn = states[(k + 1) % 2]

        def go(m):
            mine_h, mine_t = pair == m, pair == m + 20
            air = jnp.where(m == DEPTH, 2.0, 0.0)
            row = pl.ds(m - 1, 1)
            flow = [0.0, 0.0]
            for r in range(RC):
                part = pl.ds(r, 8, stride=RC)
                ghosts = cg[k, r]
                h = [H[m, r, :, half] for half in halves]
                t = [T[m, r, :, half] for half in halves]
                d = [D[m, r, :, half] for half in halves]
                gh, gt, gd = (pltpu.roll(ghosts, at - 2 * m, 1) for at in (129, 89, 49))
                tl, tr = sides(t[0], t[1], gt)
                h0, h1 = pltpu.roll(h[0], LN - 1, 1), pltpu.roll(h[1], LN - 1, 1)
                d0, d1 = pltpu.roll(d[0], LN - 1, 1), pltpu.roll(d[1], LN - 1, 1)
                f0 = (d[0] + jnp.where(final, d1, d0)) * (jnp.where(final, h1, h0) - h[0])
                f1 = (d[1] + jnp.where(final, gd, d1)) * (jnp.where(final, gh, h1) - h[1])
                s0, s1 = pltpu.roll(f0, 1, 1), pltpu.roll(f1, 1, 1)
                across = (
                    f0 - jnp.where(first, (d[0] + gd) * (h[0] - gh), s0),
                    f1 - jnp.where(first, s0, s1),
                )
                hn, tn = [], []
                for i, half in enumerate(halves):
                    hc, tc, dc = h[i], t[i], d[i]
                    if r == 0:
                        hu, tu, du = (
                            shift_rows(x[m, RC - 1, :, half], g[row, :][:, half], True)
                            for x, g in ((H, rr.at[e_in, 0, 0]), (T, rr.at[e_in, 0, 1]), (D, dr.at[e_in, 0]))
                        )
                        flow[i] = (du + dc) * (hc - hu)
                    else:
                        tu = T[m, r - 1, :, half]
                    if r == RC - 1:
                        hd, td, dd = (
                            shift_rows(x[m, 0, :, half], g[row, :][:, half], False)
                            for x, g in ((H, rr.at[e_in, 1, 0]), (T, rr.at[e_in, 1, 1]), (D, dr.at[e_in, 1]))
                        )
                    else:
                        hd, td, dd = H[m, r + 1, :, half], T[m, r + 1, :, half], D[m, r + 1, :, half]
                    below = (dc + dd) * (hd - hc)
                    out = (dc + D[m + 1, r, :, half]) * (H[m + 1, r, :, half] - hc)
                    into = (dc + D[m - 1, r, :, half]) * (H[m - 1, r, :, half] - hc)
                    moist = (out + into) + (below - flow[i]) + across[i]
                    flow[i] = below
                    total = (T[m + 1, r, :, half] + T[m - 1, r, :, half]) + (tu + td) + (tl[i] + tr[i])
                    a = xg[m - 1, i, part, :] if k == 0 else ab[m - 1, r, :, half]
                    hyd = gb[m - 1, r, :, half] * (0.85 - a)
                    h1_ = hc + moist - 0.3 * hyd
                    t1_ = tc + 0.15 * (total - 6.0 * tc) + 4.0 * hyd + air * out
                    if k < 3:
                        Hn[m, r, :, half] = h1_
                        Tn[m, r, :, half] = t1_
                        ab[m - 1, r, :, half] = a + hyd
                        dn, gn = rates(h1_, t1_)
                        Dn[m, r, :, half] = dn
                        gb[m - 1, r, :, half] = gn
                    else:
                        xh[m - 1, i, part, :] = h1_
                        xs[m - 1, i, part, :] = t1_
                    hn.append(h1_)
                    tn.append(t1_)
                if k < 3:
                    skin_pack(e, m, r, hn, tn, mine_h, mine_t)

        sweep(go, begin + 1, end + 1)
        if end == DEPTH and k < 3:
            skin_air(states[(k + 1) % 2])

    def inflow(k):
        T = states[k % 2][1]
        gain = 0.0 if k == 0 else ub[...]
        for r in range(RC):
            gain = gain + (T[0, r] - T[1, r])
        ub[...] = gain

    for e in range(2):
        for r in range(XC):
            ics[e, r] = zero
    wait(loads[0])

    def pack0(m, c):
        mine = pair == m
        for r in range(XC):
            x = [xt[m - 1, i, pl.ds(r, 8, stride=XC), :] for i in range(2)]
            for i, half in enumerate(halves):
                th0[m, r, :, half] = x[i]
            int_pack(0, m, r, x, mine)
        return c

    lax.fori_loop(1, NZ + 1, pack0, 0, unroll=2)
    pl.semaphore_wait(barrier, NB - 1 + NH - 1)
    ex_i0 = int_halo(0)
    start(ex_i0)

    col_load.wait()

    col = col_ref[...]
    owner = col >> 7
    colf = jnp.broadcast_to(owner.astype(F32), (ARCS, ARCS))
    owner_down = colf.T
    q_i = lax.broadcasted_iota(jnp.int32, (ARCS, ARCS), 0)
    p_i = lax.broadcasted_iota(jnp.int32, (ARCS, ARCS), 1)
    earlier = jnp.where((owner_down == colf) & (q_i < p_i), 1.0, 0.0)
    rank = jnp.sum(earlier, axis=0, keepdims=True).astype(jnp.int32)
    ob = col >> 9
    pos = (ob >> 3) * LN + (((ob + b) & 7) << 4) + ((owner & 3) << 2) + rank
    posf = pos.astype(F32)
    pos_down = jnp.broadcast_to(posf, (LN, ARCS)).T
    val_down = jnp.broadcast_to((col & 511).astype(F32) + 1.0, (LN, ARCS)).T
    lanes_a = lax.broadcasted_iota(jnp.int32, (ARCS, LN), 1).astype(F32)
    for t in range(4):
        hit = jnp.where(pos_down == lanes_a + float(t * LN), val_down, 0.0)
        qs[t] = jnp.broadcast_to(jnp.sum(hit, axis=0, keepdims=True) - 1.0, (8, LN))
    slot_i = lax.broadcasted_iota(jnp.int32, (4 * LN, ARCS), 0).astype(F32)
    o2[...] = jnp.where(slot_i == posf, 1.0, 0.0).astype(BF16)

    def clear(e, c):
        for side in range(2):
            for r in range(RC):
                cs[e, r] = zero
            for f in range(2):
                rs[e, side, f] = jnp.zeros((DEPTH, ARCS), F32)
        return c

    lax.fori_loop(0, N_EX, clear, 0)
    to_blk(qs, qr, q_send, q_recv)
    for i in (1, 2, 3):
        wait(loads[i])
    skin_first()
    ex_s0 = skin_halo(0)
    start(ex_s0)

    wait(loads[4])
    wait(loads[5])
    int_step(th0, th1, False)
    wait(ex_i0)
    int_place(0)
    int_fix(0, th1, False)
    ex_i1 = int_halo(1)
    start(ex_i1)
    int_step(th1, th0, True)

    wait(loads[6])
    wait(ex_s0)
    skin_place(0, 0, False)
    skin_step(0, 1, DEPTH, BULK[1], BULK[0])
    ex_b1 = skin_halo(BULK[1])
    start(ex_b1)

    wait(ex_i1)
    int_place(1)
    int_fix(1, th0, True)
    y_i = lax.broadcasted_iota(jnp.int32, (IY, LN), 0)
    c_i = lax.broadcasted_iota(jnp.int32, (IY, LN), 1)

    def mean_matrix(i):
        return jnp.where(((c_i >> 5) == i) & ((c_i & 31) == (y_i >> 3)), 1.0 / 64.0, 0.0).astype(BF16)

    coarse = jnp.zeros((NZ, LN), F32)
    for i in range(XC):
        coarse = coarse + pick(csum[i], mean_matrix(i))
    for i in range(NH):
        csend[i] = coarse[8 * i : 8 * i + 8]
    to_ha(csend, abuf, x1_send, x1_recv)

    from_blk(qs, qr, q_send, q_recv)
    slots = combine(qr)
    for t in range(4):
        key = jnp.broadcast_to(slots[t][0:1], (4 * LN, LN))
        row = lax.broadcasted_iota(jnp.int32, (4 * LN, LN), 0).astype(F32)
        oh[:, t * LN : (t + 1) * LN] = jnp.where(row == key, 1.0, 0.0).astype(BF16)

    from_ha(csend, abuf, x1_send, x1_recv)
    wide = pick(jnp.concatenate([abuf[i] for i in range(NH)], axis=1), oh[...])
    for t in range(4):
        ws[t] = wide[:, t * LN : (t + 1) * LN]
    to_blk(ws, rbuf, x2_send, x2_recv)

    wait(ex_b1)
    skin_place(1, BULK[1], False)
    skin_step(1, 2, DEPTH, BULK[2], BULK[1])
    ex_b2 = skin_halo(BULK[2])
    start(ex_b2)

    from_blk(ws, rbuf, x2_send, x2_recv)
    bound = pick(jnp.concatenate(combine(rbuf), axis=1), o2[...])
    bound_d = half_diff(jnp.ones((8, ARCS), F32), bound)
    for r in range(RC):
        for _, T, D in states:
            T[0, r] = bound
            D[0, r] = bound_d

    inflow(0)
    skin_step(0, 0, 1, WEDGE[1], BULK[0])
    ex_w1 = skin_halo(WEDGE[1])
    start(ex_w1)
    inflow(1)

    wait(ex_b2)
    skin_place(2, BULK[2], False)
    skin_step(2, 3, DEPTH, BULK[3], BULK[2])
    ex_b3 = skin_halo(BULK[3])
    start(ex_b3)

    wait(ex_w1)
    skin_place(1, WEDGE[1], True)
    skin_step(1, 0, 2, WEDGE[2], WEDGE[1])
    ex_w2 = skin_halo(WEDGE[2])
    start(ex_w2)
    inflow(2)

    wait(ex_w2)
    skin_place(2, WEDGE[2], True)
    skin_step(2, 0, 3, WEDGE[3], WEDGE[2])
    ex_w3 = skin_halo(WEDGE[3])
    start(ex_w3)
    inflow(3)
    heat = pick(0.15 * ub[...], o2[...], transpose_b=True)
    for t in range(4):
        vs[t] = heat[:, t * LN : (t + 1) * LN]
    to_blk(vs, vr, u2_send, u2_recv)

    wait(ex_b3)
    skin_place(3, BULK[3], False)
    skin_step(3, 4, DEPTH, None, BULK[3])
    wait(ex_w3)
    skin_place(3, WEDGE[3], True)

    from_blk(vs, vr, u2_send, u2_recv)
    summed = pick(jnp.concatenate(combine(vr), axis=1), oh[...], transpose_b=True)
    for i in range(NH):
        ss[i] = summed[:, i * LN : (i + 1) * LN]
    to_ha(ss, ubuf, u1_send, u1_recv)

    skin_step(3, 0, 4, None, WEDGE[3])

    from_ha(ss, ubuf, u1_send, u1_recv)
    uptake = jnp.concatenate([ubuf[i] for i in range(NH)], axis=0)
    for i in range(XC):
        ge[i] = 0.5 * pick(uptake, mean_matrix(i), transpose_b=True)

    def finish(m, c):
        for i, half in enumerate(halves):
            cool = jnp.zeros((8, LN), F32)
            for g in range(XC):
                row = jnp.broadcast_to(ge[g, pl.ds(m - 1, 1), :][:, half], (8, LN))
                cool = jnp.where((sub >> 1) == g, row, cool)
            for r in range(XC):
                xt[m - 1, i, pl.ds(r, 8, stride=XC), :] = th0[m, r, :, half] - cool
        return c

    lax.fori_loop(1, NZ + 1, finish, 0, unroll=2)


def on_device(int_temp, int_degree, int_affinity, hum, stemp, sdeg, ambient, colmap):
    vmem = pltpu.VMEM
    sem = pltpu.SemaphoreType.DMA
    skin_buf = vmem((DEPTH + 2, RC, 8, ARCS), F32)
    int_buf = vmem((NZ + 2, XC, 8, IY), F32)
    int_stage = vmem((NZ, 2, IX, LN), F32)
    skin_stage = vmem((DEPTH, 2, ROWS, LN), F32)
    outside = pl.BlockSpec(memory_space=pltpu.HBM)
    interior = jax.ShapeDtypeStruct((NZ, IX, IY), F32)
    skin = jax.ShapeDtypeStruct((DEPTH, ROWS, ARCS), F32)
    outs = (interior, interior, skin, skin)
    msg = vmem((NB, 8, LN), F32)
    tiles = vmem((4, 8, LN), F32)
    inside = pl.BlockSpec(memory_space=pltpu.VMEM)
    int_half = jax.ShapeDtypeStruct((NZ, 2, IX, LN), F32)
    skin_half = jax.ShapeDtypeStruct((DEPTH, 2, ROWS, LN), F32)
    results = pl.pallas_call(
        body,
        out_shape=(int_half, int_half, skin_half, skin_half),
        in_specs=[outside] * 8,
        out_specs=(inside,) * 4,
        scratch_shapes=[
            int_stage, skin_stage,
            vmem((2, ROWS, LN), F32), vmem((1, ARCS), jnp.int32),
            int_buf, int_buf, vmem((NZ, XC, 8, IY), F32),
            skin_buf, skin_buf, skin_buf, skin_buf, skin_buf, skin_buf,
            vmem((DEPTH, RC, 8, ARCS), F32), vmem((DEPTH, RC, 8, ARCS), F32),
            vmem((N_EX, RC, 8, LN), F32), vmem((N_EX, 2, RC, 8, LN), F32),
            vmem((N_EX, 2, 2, DEPTH, ARCS), F32), vmem((N_EX, 2, 2, DEPTH, ARCS), F32),
            vmem((4, RC, 8, LN), F32), vmem((N_EX, 2, DEPTH, ARCS), F32),
            vmem((2, XC, 8, LN), F32), vmem((2, 2, XC, 8, LN), F32), vmem((2, XC, 8, LN), F32),
            vmem((2, 2, NZ, IY), F32), vmem((2, 2, NZ, IY), F32),
            tiles, msg, vmem((4 * LN, 4 * LN), BF16), vmem((4 * LN, ARCS), BF16),
            vmem((XC, NZ, IY), F32), tiles, tiles, tiles, msg,
            vmem((8, ARCS), F32), tiles, msg, tiles, tiles,
            vmem((XC, NZ, IY), F32),
            sem((15,)), sem((N_EX + 2, 4)), sem((N_EX + 2, 4)),
            sem((NB,)), sem((NB,)), sem((NH,)), sem((NH,)),
            sem((NB,)), sem((NB,)), sem((NB,)), sem((NB,)), sem((NH,)), sem((NH,)),
        ],
        compiler_params=pltpu.CompilerParams(
            collective_id=0, has_side_effects=True, vmem_limit_bytes=50944 * 1024
        ),
        name="pylon",
    )(*(
        pltpu.with_memory_space_constraint(x, pltpu.HBM)
        for x in (int_temp, int_degree, int_affinity, hum, stemp, sdeg, ambient, colmap.reshape(1, ARCS))
    ))
    return pl.pallas_call(
        settle,
        out_shape=outs,
        in_specs=[inside] * 4,
        out_specs=(outside,) * 4,
        scratch_shapes=[sem((8,))],
        compiler_params=pltpu.CompilerParams(vmem_limit_bytes=8 * 1024 * 1024),
        name="settle",
    )(*results)


def solution(mesh):
    plan = P(None, "blk", "ha")
    band = P(None, "ha", "blk")
    return jax.shard_map(
        on_device,
        mesh=mesh,
        in_specs=(plan, plan, plan, band, band, band, P("ha", "blk"), P("blk")),
        out_specs=(plan, plan, band, band),
        check_vma=False,
    )
```
